32 devices in a mesh: wide: 8 (over z, core), narrow: 4 (over y, x).
Axes of the slice: x: 2, y: 2, z: 4, core: 2. Of those that a mesh axis runs over, the one named last changes fastest.
Arguments:
- a_blocks: float32 [4, 48, 128, 128], P('narrow', 'wide'), may hold values from -1.2 to 1.2
- a_index: int32 [4, 2, 48], P('narrow', None, 'wide'), may hold values from -1 to 1023, as said below
- b_blocks: float32 [4, 192, 128, 128], P('narrow', 'wide'), may hold values from -1.2 to 1.2
- b_index: int32 [4, 2, 192], P('narrow', None, 'wide'), may hold values from -1 to 1023, as said below
Outputs:
- product: float32 [4, 2, 8, 4, 128, 128], P('narrow', None, 'wide')
The draws below stay inside these ranges and needn't reach their ends.
Inputs may be any that keep to these rules, and one draw needn't show every extreme that they name: Slot s of a_index[r] is empty, with both entries -1, or names a block row congruent to r modulo 4 and a block column congruent to s // 6 modulo 8; no block is named twice. Slot s of b_index[r] is empty, with both entries -1, or names a block row congruent to r modulo 4 and a window block column congruent to s // 24 modulo 8; no block is named twice.
All inputs are finite; a program needn't handle non-finite values.
Results may differ from the reference program's by a relative error of at most 0.0001.
Values sent between devices are 32-bit elements; how exact they have to be, the bound alone decides.
No kernel may reach another device: no remote copies, remote signals or barrier semaphores. Data moves between devices by JAX's collectives and lax.ppermute only.
A program may use at most 128 MiB of HBM per device.

```python
import jax
import jax.numpy as jnp
from jax import lax

BS = 128
KBLOCKS = 1024
TA = 3
RL = 2
CL = 4
TB = 6
BAND = 24
NR = 8
NC = 32
SA = 6
SB = 24
N_WIDE = 8
N_NARROW = 4


def device_thresholds(key, devices):
    busy_key, empty_key, rate_key = jax.random.split(key, 3)
    busiest = jax.random.randint(busy_key, (), 0, devices)
    offset_by = jax.random.randint(empty_key, (), 1, devices)
    thresholds = jax.random.randint(rate_key, (devices,), 3, 8)
    device_ids = jnp.arange(devices)
    thresholds = jnp.where(device_ids == busiest, 8, thresholds)
    thresholds = jnp.where(device_ids == (busiest + offset_by) % devices, 0, thresholds)
    return thresholds


def finish_slots(key, rows, cols, keep, narrow_count, wide_count, slots):
    rows = jnp.where(keep, rows, -1).reshape(narrow_count, wide_count, slots)
    cols = jnp.where(keep, cols, -1).reshape(narrow_count, wide_count, slots)
    scores = jax.random.randint(key, (narrow_count, wide_count, slots), 0, 1 << 20) * slots + jnp.arange(slots)
    order = jnp.argsort(scores, axis=-1, stable=True)
    rows = jnp.take_along_axis(rows, order, axis=-1)
    cols = jnp.take_along_axis(cols, order, axis=-1)
    stacked = jnp.stack([rows, cols], axis=2)
    return stacked.transpose(0, 2, 1, 3).reshape(narrow_count, 2, wide_count * slots).astype(jnp.int32)


def draw_a_index(key, part):
    key = jax.random.fold_in(key, 101)
    rate_key, coin_key, order_key = jax.random.split(key, 3)
    narrow_count = N_NARROW
    wide_count = N_WIDE
    half_band = BAND // 2
    narrow_ids = jnp.arange(narrow_count)[:, None, None, None]
    wide_ids = jnp.arange(wide_count)[None, :, None, None]
    line_ids = jnp.arange(RL)[None, None, :, None]
    candidate = jnp.arange(TA)[None, None, None, :]
    full_shape = (narrow_count, wide_count, RL, TA)
    window_row = jnp.broadcast_to(line_ids * narrow_count + narrow_ids, full_shape)
    diagonal_k = jnp.mod(KBLOCKS - NR // 2 + window_row, KBLOCKS)
    lowest = diagonal_k - half_band
    first_k = lowest + jnp.mod(wide_ids - lowest, wide_count)
    inner_k = jnp.mod(first_k + candidate * wide_count, KBLOCKS)
    thresholds = device_thresholds(rate_key, narrow_count * wide_count).reshape(narrow_count, wide_count, 1, 1)
    coin_toss = jax.random.randint(coin_key, full_shape, 0, 8)
    keep = (coin_toss < thresholds) | (inner_k == diagonal_k)
    return finish_slots(order_key, window_row, inner_k, keep, narrow_count, wide_count, SA)


def draw_b_index(key, part):
    key = jax.random.fold_in(key, 202)
    rate_key, coin_key, order_key = jax.random.split(key, 3)
    narrow_count = N_NARROW
    wide_count = N_WIDE
    half_band = BAND // 2
    narrow_ids = jnp.arange(narrow_count)[:, None, None, None]
    wide_ids = jnp.arange(wide_count)[None, :, None, None]
    line_ids = jnp.arange(CL)[None, None, :, None]
    candidate = jnp.arange(TB)[None, None, None, :]
    full_shape = (narrow_count, wide_count, CL, TB)
    window_col = jnp.broadcast_to(line_ids * wide_count + wide_ids, full_shape)
    diagonal_k = jnp.mod(KBLOCKS - NC // 2 + window_col, KBLOCKS)
    lowest = diagonal_k - half_band
    first_k = lowest + jnp.mod(narrow_ids - lowest, narrow_count)
    inner_k = jnp.mod(first_k + candidate * narrow_count, KBLOCKS)
    thresholds = device_thresholds(rate_key, narrow_count * wide_count).reshape(narrow_count, wide_count, 1, 1)
    coin_toss = jax.random.randint(coin_key, full_shape, 0, 8)
    keep = (coin_toss < thresholds) | (inner_k == diagonal_k)
    return finish_slots(order_key, inner_k, window_col, keep, narrow_count, wide_count, SB)


def steps_of(own_key, dims, cuts, least, high):
    def one(dim, parts):
        draws = jax.random.uniform(jax.random.fold_in(jax.random.fold_in(own_key, 6), dim), (parts,), jnp.float32, least / len(cuts), high / len(cuts))
        return jnp.repeat(jnp.exp(draws), dims[dim] // parts).reshape((-1,) + (1,) * (len(dims) - dim - 1))

    factor_of = one(*cuts[0])
    for cut in cuts[1:]:
        factor_of = factor_of * one(*cut)
    return factor_of


def noise(own_key, shape, deviation, bound, shards=(), kind=jnp.bfloat16):
    level = steps_of(own_key, shape, shards, -0.22, 0.18) if shards else 1.0
    values = jax.random.normal(own_key, shape, jnp.float32) * deviation * level
    return jnp.minimum(jnp.maximum(values, -bound), bound).astype(kind)


def setup_inputs(seed: int = 0) -> dict:
    key_list = jax.random.split(jax.random.key(seed), 5)
    return {
        "a_blocks": noise(key_list[0], (N_NARROW, N_WIDE * SA, BS, BS), 0.15, 1.2, ((0, 4), (1, 8)), jnp.float32),
        "a_index": draw_a_index(jax.random.fold_in(key_list[4], 71), 0),
        "b_blocks": noise(key_list[2], (N_NARROW, N_WIDE * SB, BS, BS), 0.15, 1.2, ((0, 4), (1, 8)), jnp.float32),
        "b_index": draw_b_index(jax.random.fold_in(key_list[4], 71), 0),
    }


def reference(a_blocks, a_index, b_blocks, b_index):
    edge = a_blocks.shape[-1]
    first_vals = a_blocks.reshape(-1, edge, edge)
    first_rows = a_index[:, 0, :].reshape(-1)
    first_cols = a_index[:, 1, :].reshape(-1)
    second_vals = b_blocks.reshape(-1, edge, edge)
    second_rows = b_index[:, 0, :].reshape(-1)
    second_cols = b_index[:, 1, :].reshape(-1)
    slot_count = first_rows.shape[0]
    usable_first = first_rows >= 0
    table = jnp.zeros((NR, KBLOCKS), jnp.int32).at[
        jnp.where(usable_first, first_rows, NR).astype(jnp.int32),
        jnp.where(usable_first, first_cols, 0).astype(jnp.int32)].set(
        jnp.arange(1, slot_count + 1, dtype=jnp.int32), mode="drop")
    window = jnp.zeros((NR, NC, edge, edge), jnp.float32)

    def visit(position, window):
        inner_k = second_rows[position]
        column = second_cols[position]
        usable = inner_k >= 0
        slots = jnp.take(table, jnp.maximum(inner_k, 0), axis=1)
        present = (slots > 0) & usable
        row_panel = jnp.take(first_vals, jnp.maximum(slots - 1, 0), axis=0) * present[:, None, None].astype(jnp.float32)
        partial_value = jnp.einsum('lxy,yz->lxz', row_panel, second_vals[position], precision=lax.Precision.HIGHEST)
        return window.at[:, jnp.maximum(column, 0)].add(partial_value)

    window = lax.fori_loop(0, second_rows.shape[0], visit, window)
    return window.reshape(RL, N_NARROW, CL, N_WIDE, edge, edge).transpose(1, 0, 3, 2, 4, 5)
```

```python
import functools

import jax
import jax.numpy as jnp
from jax import lax
from jax.experimental import pallas as pl
from jax.experimental.pallas import tpu as pltpu
from jax.sharding import PartitionSpec as P

RL = 2
CL = 4
KBLOCKS = 1024
PAD = 8
AXES = ("wide", "narrow")
VMEM_LIMIT = 32 * 1024 * 1024


def split(value):
    high = value.astype(jnp.bfloat16)
    low = (value - high.astype(jnp.float32)).astype(jnp.bfloat16)
    return high, low


def split_kernel(b_ref, high_ref, low_ref):
    slots, edge = b_ref.shape[0], b_ref.shape[2]

    def one(slot, _):
        high, low = split(b_ref[slot])
        rows = pl.ds(pl.multiple_of(slot * edge, edge), edge)
        high_ref[rows, :] = high
        low_ref[rows, :] = low
        return 0

    lax.fori_loop(0, slots, one, 0)
    high_ref[slots * edge :, :] = jnp.zeros((edge, edge), jnp.bfloat16)
    low_ref[slots * edge :, :] = jnp.zeros((edge, edge), jnp.bfloat16)


def split_blocks(b_blocks):
    slots, edge, _ = b_blocks.shape
    shape = jax.ShapeDtypeStruct(((slots + 1) * edge, edge), jnp.bfloat16)
    return pl.pallas_call(
        split_kernel,
        out_shape=(shape, shape),
        compiler_params=pltpu.CompilerParams(vmem_limit_bytes=VMEM_LIMIT),
    )(b_blocks)


def product_kernel(
    edge, slots, table_ref, one_ref, two_ref, high_ref, low_ref, out_ref,
    a_ref, index_ref, left_high, left_low, right_high, right_low, block_sems, index_sems,
):
    shares = (one_ref, two_ref)
    rows = slots * edge
    index_copies = [
        pltpu.make_async_copy(ref.at[pl.ds(rows, PAD)], index_ref.at[n], index_sems.at[n])
        for n, ref in enumerate(shares)
    ]
    block_copies = [
        pltpu.make_async_copy(ref.at[pl.ds(0, rows)], a_ref.at[n], block_sems.at[n])
        for n, ref in enumerate(shares)
    ]
    for copy in index_copies + block_copies:
        copy.start()
    for copy in index_copies:
        copy.wait()
    for n in range(len(shares)):
        for slot in range(slots):
            at = (n * slots + slot) * edge
            inner = index_ref[n, 1, slot].astype(jnp.int32)
            for m in range(CL):
                block = table_ref[inner * CL + m]
                source = pl.ds(pl.multiple_of(block * edge, edge), edge)
                right_high[at : at + edge, m * edge : (m + 1) * edge] = high_ref[source, :]
                right_low[at : at + edge, m * edge : (m + 1) * edge] = low_ref[source, :]
    left_high[...] = jnp.zeros_like(left_high)
    left_low[...] = jnp.zeros_like(left_low)
    for copy in block_copies:
        copy.wait()
    for n in range(len(shares)):
        for slot in range(slots):
            at = (n * slots + slot) * edge
            line = index_ref[n, 0, slot].astype(jnp.int32)
            high, low = split(a_ref[n, slot * edge : (slot + 1) * edge, :])
            target = pl.ds(pl.multiple_of(line * edge, edge), edge)
            left_high[target, at : at + edge] = high
            left_low[target, at : at + edge] = low
    dot = functools.partial(jnp.dot, preferred_element_type=jnp.float32)
    for m in range(0, CL, 2):
        columns = slice(m * edge, (m + 2) * edge)
        value = (
            dot(left_high[...], right_high[:, columns])
            + dot(left_low[...], right_high[:, columns])
            + dot(left_high[...], right_low[:, columns])
        )
        for l in range(RL):
            for n in range(2):
                out_ref[l * CL + m + n] = value[l * edge : (l + 1) * edge, n * edge : (n + 1) * edge]


def product(table, one, two, high, low, slots):
    edge = high.shape[1]
    depth = 2 * slots * edge
    return pl.pallas_call(
        functools.partial(product_kernel, edge, slots),
        out_shape=jax.ShapeDtypeStruct((RL * CL, edge, edge), jnp.float32),
        in_specs=[
            pl.BlockSpec(memory_space=pltpu.SMEM),
            pl.BlockSpec(memory_space=pl.ANY),
            pl.BlockSpec(memory_space=pl.ANY),
            pl.BlockSpec(memory_space=pltpu.VMEM),
            pl.BlockSpec(memory_space=pltpu.VMEM),
        ],
        out_specs=pl.BlockSpec(memory_space=pltpu.VMEM),
        scratch_shapes=[
            pltpu.VMEM((2, slots * edge, edge), jnp.float32),
            pltpu.SMEM((2, PAD, edge), jnp.float32),
            pltpu.VMEM((RL * edge, depth), jnp.bfloat16),
            pltpu.VMEM((RL * edge, depth), jnp.bfloat16),
            pltpu.VMEM((depth, CL * edge), jnp.bfloat16),
            pltpu.VMEM((depth, CL * edge), jnp.bfloat16),
            pltpu.SemaphoreType.DMA((2,)),
            pltpu.SemaphoreType.DMA((2,)),
        ],
        compiler_params=pltpu.CompilerParams(vmem_limit_bytes=VMEM_LIMIT),
        cost_estimate=pl.CostEstimate(
            flops=6 * RL * depth * CL * edge * edge, bytes_accessed=4 * 1024 * 1024, transcendentals=0
        ),
    )(table, one, two, high, low)


def local(a_blocks, a_index, b_blocks, b_index):
    narrow = lax.axis_size("narrow")
    wide = lax.axis_size("wide")
    slots = a_blocks.shape[1]
    edge = a_blocks.shape[-1]
    slots_second = b_blocks.shape[1]

    def device(row, column):
        return column * narrow + row

    stored = a_index[0, 0] >= 0
    line = jnp.where(stored, a_index[0, 0] // narrow, 0)
    inner = jnp.where(stored, a_index[0, 1] // narrow, KBLOCKS // narrow)
    index = jnp.stack([line, inner]).astype(jnp.float32)
    index = jnp.pad(index, ((0, PAD - 2), (0, edge - slots)))
    share = jnp.concatenate([a_blocks.reshape(slots * edge, edge), index], axis=0)

    table = jnp.arange((KBLOCKS // narrow + 1) * CL)[:, None]
    wanted = b_index[0, 0] // narrow * CL + b_index[0, 1] // wide
    hit = (table == wanted[None, :]) & (b_index[0, 0] >= 0)[None, :]
    table = slots_second + jnp.sum(jnp.where(hit, jnp.arange(slots_second)[None, :] - slots_second, 0), axis=1)
    table = table.astype(jnp.int32)
    high, low = split_blocks(b_blocks[0])

    total = None
    for step in range(narrow):
        spread = []
        for column in range(wide):
            target = column % narrow
            half = column // narrow
            for row in range(narrow):
                plane = row ^ target ^ step
                spread.append((device(row, column), device(target, plane * 2 + half)))
        mine = lax.ppermute(share, AXES, spread)
        swap = [(device(r, c), device(r, c ^ 1)) for r in range(narrow) for c in range(wide)]
        other = lax.ppermute(mine, AXES, swap)
        partial_value = product(table, mine, other, high, low, slots)
        back = [
            (device(r, c), device(r ^ (c // 2) ^ step, c)) for r in range(narrow) for c in range(wide)
        ]
        got = lax.ppermute(partial_value, AXES, back)
        total = got if total is None else total + got
    return total.reshape(1, RL, 1, CL, edge, edge)


def solution(mesh):
    return jax.shard_map(
        local,
        mesh=mesh,
        in_specs=(
            P("narrow", "wide", None, None),
            P("narrow", None, "wide"),
            P("narrow", "wide", None, None),
            P("narrow", None, "wide"),
        ),
        out_specs=P("narrow", None, "wide", None, None, None),
        check_vma=False,
    )
```

```python
import functools

import jax
import jax.numpy as jnp
from jax import lax
from jax.experimental import pallas as pl
from jax.experimental.pallas import tpu as pltpu
from jax.sharding import PartitionSpec as P

RL = 2
CL = 4
KBLOCKS = 1024
PAD = 8
AXES = ("wide", "narrow")
VMEM_LIMIT = 32 * 1024 * 1024


def split(value):
    high = value.astype(jnp.bfloat16)
    low = (value - high.astype(jnp.float32)).astype(jnp.bfloat16)
    return high, low


def product_kernel(edge, slots, has_start, *refs):
    pick_ref, table_ref, mine_one, mine_two, other_one, other_two, b_hbm = refs[:7]
    refs = refs[7:]
    if has_start:
        start_ref, refs = refs[0], refs[1:]
    (out_ref, a_ref, index_ref, b_ref, left_high, left_low, right_high, right_low,
     block_sems, index_sems, b_sem) = refs
    rows = slots * edge
    slots_second = b_hbm.shape[0]
    b_copy = pltpu.make_async_copy(b_hbm, b_ref.at[pl.ds(0, slots_second)], b_sem)

    def copies(n, ref):
        return (
            pltpu.make_async_copy(ref.at[pl.ds(rows, PAD)], index_ref.at[n], index_sems.at[n]),
            pltpu.make_async_copy(ref.at[pl.ds(0, rows)], a_ref.at[n], block_sems.at[n]),
        )

    for n, (mine, other) in enumerate(((mine_one, other_one), (mine_two, other_two))):
        @pl.when(pick_ref[0] == 0)
        def _():
            for copy in copies(n, mine):
                copy.start()

        @pl.when(pick_ref[0] != 0)
        def _():
            for copy in copies(n, other):
                copy.start()

    b_copy.start()
    b_ref[slots_second] = jnp.zeros((edge, edge), jnp.float32)
    left_high[...] = jnp.zeros_like(left_high)
    left_low[...] = jnp.zeros_like(left_low)
    waits = [copies(n, ref) for n, ref in enumerate((mine_one, mine_two))]
    for index_copy, block_copy in waits:
        index_copy.wait()
        block_copy.wait()
    for n in range(2):
        for slot in range(slots):
            at = (n * slots + slot) * edge
            line = index_ref[n, 0, slot].astype(jnp.int32)
            high, low = split(a_ref[n, slot * edge : (slot + 1) * edge, :])
            target = pl.ds(pl.multiple_of(line * edge, edge), edge)
            left_high[target, at : at + edge] = high
            left_low[target, at : at + edge] = low
    b_copy.wait()
    for n in range(2):
        for slot in range(slots):
            at = (n * slots + slot) * edge
            inner = index_ref[n, 1, slot].astype(jnp.int32)
            for m in range(CL):
                high, low = split(b_ref[table_ref[inner * CL + m]])
                right_high[at : at + edge, m * edge : (m + 1) * edge] = high
                right_low[at : at + edge, m * edge : (m + 1) * edge] = low
    dot = functools.partial(jnp.dot, preferred_element_type=jnp.float32)
    for m in range(0, CL, 2):
        columns = slice(m * edge, (m + 2) * edge)
        value = (
            dot(left_high[...], right_high[:, columns])
            + dot(left_low[...], right_high[:, columns])
            + dot(left_high[...], right_low[:, columns])
        )
        for l in range(RL):
            for n in range(2):
                at = l * CL + m + n
                piece = value[l * edge : (l + 1) * edge, n * edge : (n + 1) * edge]
                out_ref[at] = start_ref[at] + piece if has_start else piece


def product(pick, table, mine, other, b_blocks, start=None):
    slots_second, edge, _ = b_blocks.shape
    slots = (mine[0].shape[0] - PAD) // edge
    depth = 2 * slots * edge
    anywhere = pl.BlockSpec(memory_space=pl.ANY)
    operands = [pick, table, *mine, *other, b_blocks] + ([] if start is None else [start])
    return pl.pallas_call(
        functools.partial(product_kernel, edge, slots, start is not None),
        out_shape=jax.ShapeDtypeStruct((RL * CL, edge, edge), jnp.float32),
        in_specs=[pl.BlockSpec(memory_space=pltpu.SMEM)] * 2
        + [anywhere] * 5
        + ([] if start is None else [pl.BlockSpec(memory_space=pltpu.VMEM)]),
        out_specs=pl.BlockSpec(memory_space=pltpu.VMEM),
        scratch_shapes=[
            pltpu.VMEM((2, slots * edge, edge), jnp.float32),
            pltpu.SMEM((2, PAD, edge), jnp.float32),
            pltpu.VMEM((slots_second + 1, edge, edge), jnp.float32),
            pltpu.VMEM((RL * edge, depth), jnp.bfloat16),
            pltpu.VMEM((RL * edge, depth), jnp.bfloat16),
            pltpu.VMEM((depth, CL * edge), jnp.bfloat16),
            pltpu.VMEM((depth, CL * edge), jnp.bfloat16),
            pltpu.SemaphoreType.DMA((2,)),
            pltpu.SemaphoreType.DMA((2,)),
            pltpu.SemaphoreType.DMA,
        ],
        compiler_params=pltpu.CompilerParams(vmem_limit_bytes=VMEM_LIMIT),
        cost_estimate=pl.CostEstimate(
            flops=6 * RL * depth * CL * edge * edge, bytes_accessed=4 * 1024 * 1024, transcendentals=0
        ),
    )(*operands)


def block_table(b_index, narrow, wide):
    slots_second = b_index.shape[-1]
    table = jnp.arange((KBLOCKS // narrow + 1) * CL)[:, None]
    wanted = b_index[0, 0] // narrow * CL + b_index[0, 1] // wide
    hit = (table == wanted[None, :]) & (b_index[0, 0] >= 0)[None, :]
    found = jnp.where(hit, jnp.arange(slots_second)[None, :] - slots_second, 0)
    return (slots_second + jnp.sum(found, axis=1)).astype(jnp.int32)


def local(a_blocks, a_index, b_blocks, b_index):
    narrow = lax.axis_size("narrow")
    wide = lax.axis_size("wide")
    groups = narrow // 2
    planes = wide // 2
    slots = a_blocks.shape[1]
    edge = a_blocks.shape[-1]
    row = lax.axis_index("narrow")
    column = lax.axis_index("wide")
    kind = (row // 2) ^ (column // 2 % groups)

    def permute(value, to):
        pairs = []
        for r in range(narrow):
            for c in range(wide):
                target = to(r, c)
                if target is not None:
                    pairs.append((c * narrow + r, target[1] * narrow + target[0]))
        return lax.ppermute(value, AXES, pairs)

    def swap(value):
        return permute(value, lambda r, c: (r, c ^ 1))

    second = b_blocks[0]
    second_other = permute(second, lambda r, c: (r ^ 1, c))
    index_other = permute(b_index, lambda r, c: (r ^ 1, c))

    stored = a_index[0, 0] >= 0
    line = jnp.where(stored, a_index[0, 0] // narrow, 0)
    inner = jnp.where(stored, a_index[0, 1] // narrow, KBLOCKS // narrow)
    index = jnp.stack([line, inner]).astype(jnp.float32)
    index = jnp.pad(index, ((0, PAD - 2), (0, edge - slots)))
    share = jnp.concatenate([a_blocks.reshape(slots * edge, edge), index], axis=0)

    table_own = block_table(b_index, narrow, wide)
    table_other = block_table(index_other, narrow, wide)
    pick_own = (column % 2 ^ row % 2).reshape(1)
    pick_other = 1 - pick_own

    def spread(change, step):
        def to(r, c):
            plane = c // 2
            u = plane % groups
            if (r // 2) ^ u != change:
                return None
            if change == 0 and step == 0:
                return None
            return (u * 2 + r % 2, (plane ^ step) * 2 + c % 2)
        return permute(share, to)

    def gathered(change):
        result = []
        for half in range(planes // groups):
            value = None
            for step in range(groups):
                got = share if change == 0 and step == 0 and half == 0 else spread(change, half * groups + step)
                value = got if value is None else jnp.where(kind == step, got, value)
            result.append(value)
        return result

    def window(mine, other):
        value = product(pick_own, table_own, mine, other, second)
        return product(pick_other, table_other, mine, other, second_other, value)

    moved = []
    for change in range(1, groups):
        mine = gathered(change)
        moved.append((change, mine, [swap(value) for value in mine]))
    mine = gathered(0)
    other = [swap(value) for value in mine]
    received = []
    for change, mine_moved, other_moved in moved:
        value = window(mine_moved, other_moved)
        received.append(permute(value, lambda r, c: (r ^ (change * 2), c)))
    total = window(mine, other)
    for value in received:
        total = total + value
    return total.reshape(1, RL, 1, CL, edge, edge)


def solution(mesh):
    return jax.shard_map(
        local,
        mesh=mesh,
        in_specs=(
            P("narrow", "wide", None, None),
            P("narrow", None, "wide"),
            P("narrow", "wide", None, None),
            P("narrow", None, "wide"),
        ),
        out_specs=P("narrow", None, "wide", None, None, None),
        check_vma=False,
    )
```

```python
import functools

import jax
import jax.numpy as jnp
from jax import lax
from jax.experimental import pallas as pl
from jax.experimental.pallas import tpu as pltpu
from jax.sharding import PartitionSpec as P

RL = 2
CL = 4
KBLOCKS = 1024
PAD = 8
AXES = ("wide", "narrow")
VMEM_LIMIT = 32 * 1024 * 1024


def split(value):
    high = value.astype(jnp.bfloat16)
    low = (value - high.astype(jnp.float32)).astype(jnp.bfloat16)
    return high, low


def product_kernel(edge, slots, items, choices, *refs):
    pick_ref, tables, refs = refs[0], refs[1:3], refs[3:]
    shares = [refs[n * choices : (n + 1) * choices] for n in range(items)]
    refs = refs[items * choices :]
    (b_one, b_two, out_ref, a_ref, index_ref, b_ref, left_high, left_low, right_high, right_low,
     block_sems, index_sems, b_sems) = refs
    rows = slots * edge
    slots_second = b_one.shape[0]
    b_copies = [
        pltpu.make_async_copy(ref, b_ref.at[n, pl.ds(0, slots_second)], b_sems.at[n])
        for n, ref in enumerate((b_one, b_two))
    ]

    def copies(n, ref):
        return (
            pltpu.make_async_copy(ref.at[pl.ds(rows, PAD)], index_ref.at[n], index_sems.at[n]),
            pltpu.make_async_copy(ref.at[pl.ds(0, rows)], a_ref.at[n], block_sems.at[n]),
        )

    for n in range(items):
        for choice in range(choices):
            @pl.when(pick_ref[n] == choice)
            def _():
                for copy in copies(n, shares[n][choice]):
                    copy.start()
    for copy in b_copies:
        copy.start()
    for n in range(2):
        b_ref[n, slots_second] = jnp.zeros((edge, edge), jnp.float32)
    left_high[...] = jnp.zeros_like(left_high)
    left_low[...] = jnp.zeros_like(left_low)
    dot = functools.partial(jnp.dot, preferred_element_type=jnp.float32)
    for n in range(items):
        for copy in copies(n, shares[n][0]):
            copy.wait()
        for slot in range(slots):
            at = slot * edge
            line = index_ref[n, 0, slot].astype(jnp.int32)
            high, low = split(a_ref[n, at : at + edge, :])
            target = pl.ds(pl.multiple_of(line * edge, edge), edge)
            left_high[n, target, at : at + edge] = high
            left_low[n, target, at : at + edge] = low
        which = n // (items // 2)
        if n % (items // 2) == 0:
            b_copies[which].wait()
        for slot in range(slots):
            at = slot * edge
            inner = index_ref[n, 1, slot].astype(jnp.int32)
            for m in range(CL):
                high, low = split(b_ref[which, tables[which][inner * CL + m]])
                right_high[n, at : at + edge, m * edge : (m + 1) * edge] = high
                right_low[n, at : at + edge, m * edge : (m + 1) * edge] = low
        for m in range(0, CL, 2):
            columns = slice(m * edge, (m + 2) * edge)
            value = (
                dot(left_high[n], right_high[n, :, columns])
                + dot(left_low[n], right_high[n, :, columns])
                + dot(left_high[n], right_low[n, :, columns])
            )
            for l in range(RL):
                for k in range(2):
                    at = l * CL + m + k
                    piece = value[l * edge : (l + 1) * edge, k * edge : (k + 1) * edge]
                    out_ref[at] = piece if n == 0 else out_ref[at] + piece


def product(pick, tables, shares, seconds):
    slots_second, edge, _ = seconds[0].shape
    items = len(shares)
    choices = len(shares[0])
    slots = (shares[0][0].shape[0] - PAD) // edge
    depth = slots * edge
    anywhere = pl.BlockSpec(memory_space=pl.ANY)
    return pl.pallas_call(
        functools.partial(product_kernel, edge, slots, items, choices),
        out_shape=jax.ShapeDtypeStruct((RL * CL, edge, edge), jnp.float32),
        in_specs=[pl.BlockSpec(memory_space=pltpu.SMEM)] * 3 + [anywhere] * (items * choices + 2),
        out_specs=pl.BlockSpec(memory_space=pltpu.VMEM),
        scratch_shapes=[
            pltpu.VMEM((items, depth, edge), jnp.float32),
            pltpu.SMEM((items, PAD, edge), jnp.float32),
            pltpu.VMEM((2, slots_second + 1, edge, edge), jnp.float32),
            pltpu.VMEM((items, RL * edge, depth), jnp.bfloat16),
            pltpu.VMEM((items, RL * edge, depth), jnp.bfloat16),
            pltpu.VMEM((items, depth, CL * edge), jnp.bfloat16),
            pltpu.VMEM((items, depth, CL * edge), jnp.bfloat16),
            pltpu.SemaphoreType.DMA((items,)),
            pltpu.SemaphoreType.DMA((items,)),
            pltpu.SemaphoreType.DMA((2,)),
        ],
        compiler_params=pltpu.CompilerParams(vmem_limit_bytes=VMEM_LIMIT),
        cost_estimate=pl.CostEstimate(
            flops=6 * items * RL * depth * CL * edge * edge, bytes_accessed=6 * 1024 * 1024, transcendentals=0
        ),
    )(pick, *tables, *[ref for share in shares for ref in share], *seconds)


def block_table(b_index, narrow, wide):
    slots_second = b_index.shape[-1]
    table = jnp.arange((KBLOCKS // narrow + 1) * CL)[:, None]
    wanted = b_index[0, 0] // narrow * CL + b_index[0, 1] // wide
    hit = (table == wanted[None, :]) & (b_index[0, 0] >= 0)[None, :]
    found = jnp.where(hit, jnp.arange(slots_second)[None, :] - slots_second, 0)
    return (slots_second + jnp.sum(found, axis=1)).astype(jnp.int32)


def local(a_blocks, a_index, b_blocks, b_index):
    narrow = lax.axis_size("narrow")
    wide = lax.axis_size("wide")
    groups = narrow // 2
    planes = wide // 2
    slots = a_blocks.shape[1]
    edge = a_blocks.shape[-1]
    row = lax.axis_index("narrow")
    column = lax.axis_index("wide")
    kind = (row // 2) ^ (column // 2 % groups)

    def permute(name, value, to):
        pairs = []
        for r in range(narrow):
            for c in range(wide):
                target = to(r, c)
                if target is not None:
                    pairs.append((c * narrow + r, target[1] * narrow + target[0]))
        with jax.named_scope(name):
            return lax.ppermute(value, AXES, pairs)

    def swap(name, value):
        return permute(name, value, lambda r, c: (r, c ^ 1))

    second = b_blocks[0]
    index_other = permute("second_index", b_index, lambda r, c: (r ^ 1, c))
    second_other = permute("second", second, lambda r, c: (r ^ 1, c))

    stored = a_index[0, 0] >= 0
    line = jnp.where(stored, a_index[0, 0] // narrow, 0)
    inner = jnp.where(stored, a_index[0, 1] // narrow, KBLOCKS // narrow)
    index = jnp.stack([line, inner]).astype(jnp.float32)
    index = jnp.pad(index, ((0, PAD - 2), (0, edge - slots)))
    share = jnp.concatenate([a_blocks.reshape(slots * edge, edge), index], axis=0)
    share, index_other = lax.optimization_barrier((share, index_other))

    tables = (block_table(b_index, narrow, wide), block_table(index_other, narrow, wide))

    def spread(half, share, turn):
        def to(r, c):
            plane = c // 2
            u = plane % groups
            change = (r // 2) ^ u
            return (u * 2 + r % 2, (plane ^ change ^ turn) * 2 + c % 2)
        return permute(f"share_{half}_{turn}", share, to)

    far = permute("far", share, lambda r, c: (r, (c // 2 ^ groups) * 2 + c % 2))
    turns = [[spread(half, value, turn) for turn in range(groups)] for half, value in enumerate((share, far))]
    swapped = [[swap(f"swap_{half}", value) for value in values] for half, values in enumerate(turns)]
    candidates = [[ref for pair in zip(*values) for ref in pair] for values in zip(turns, swapped)]
    crossed = (column ^ row) % 2

    def window(change):
        at = (kind ^ change) * 2
        pick = jnp.stack([at + crossed, at + crossed, at + 1 - crossed, at + 1 - crossed])
        return product(pick, tables, candidates * 2, (second, second_other))

    received = []
    for change in range(1, groups):
        value = window(change)
        received.append(permute(f"window_{change}", value, lambda r, c: (r ^ (change * 2), c)))
    total = window(0)
    for value in received:
        total = total + value
    return total.reshape(1, RL, 1, CL, edge, edge)


def solution(mesh):
    return jax.shard_map(
        local,
        mesh=mesh,
        in_specs=(
            P("narrow", "wide", None, None),
            P("narrow", None, "wide"),
            P("narrow", "wide", None, None),
            P("narrow", None, "wide"),
        ),
        out_specs=P("narrow", None, "wide", None, None, None),
        check_vma=False,
    )
```

```python
import functools

import jax
import jax.numpy as jnp
from jax import lax
from jax.experimental import pallas as pl
from jax.experimental.pallas import tpu as pltpu
from jax.sharding import PartitionSpec as P

RL = 2
CL = 4
KBLOCKS = 1024
PAD = 8
AXES = ("wide", "narrow")
VMEM_LIMIT = 16 * 1024 * 1024


def split(value):
    high = value.astype(jnp.bfloat16)
    low = (value - high.astype(jnp.float32)).astype(jnp.bfloat16)
    return high, low


def product_kernel(edge, slots, narrow, change, crossing, items, choices, has_start, *refs):
    table_ref, refs = refs[0], refs[1:]
    row, column = lax.axis_index("narrow"), lax.axis_index("wide")
    turn = (row // 2) ^ (column // 2 % (choices // 2)) ^ change
    pick = turn * 2 + ((row ^ column) % 2 ^ crossing)
    shares = [refs[n * choices : (n + 1) * choices] for n in range(items)]
    refs = refs[items * choices :]
    b_ref, refs = refs[0], refs[1:]
    if has_start:
        start_ref, refs = refs[0], refs[1:]
    out_ref, a_ref, index_ref, left_high, left_low, right_high, right_low, block_sems, index_sems = refs
    rows = slots * edge
    last = b_ref.shape[0] - 1

    def copies(n, ref):
        return (
            pltpu.make_async_copy(ref.at[pl.ds(rows, PAD)], index_ref.at[n], index_sems.at[n]),
            pltpu.make_async_copy(ref.at[pl.ds(0, rows)], a_ref.at[n], block_sems.at[n]),
        )

    for n in range(items):
        for choice in range(choices):
            @pl.when(pick == choice)
            def _():
                for copy in copies(n, shares[n][choice]):
                    copy.start()
    left_high[...] = jnp.zeros_like(left_high)
    left_low[...] = jnp.zeros_like(left_low)
    waits = [copies(n, shares[n][0]) for n in range(items)]
    for index_copy, _ in waits:
        index_copy.wait()
    for n in range(items):
        for slot in range(slots):
            at = (n * slots + slot) * edge
            inner = index_ref[n, 1, slot].astype(jnp.int32)
            inner = jnp.where(inner < 0, KBLOCKS // narrow, lax.div(jnp.maximum(inner, 0), narrow))
            for m in range(CL):
                block = table_ref[inner * CL + m]
                high, low = split(jnp.where(block <= last, b_ref[jnp.minimum(block, last)], 0.0))
                right_high[at : at + edge, m * edge : (m + 1) * edge] = high
                right_low[at : at + edge, m * edge : (m + 1) * edge] = low
    for _, block_copy in waits:
        block_copy.wait()
    for n in range(items):
        for slot in range(slots):
            at = (n * slots + slot) * edge
            line = lax.div(jnp.maximum(index_ref[n, 0, slot].astype(jnp.int32), 0), narrow)
            high, low = split(a_ref[n, slot * edge : (slot + 1) * edge, :])
            target = pl.ds(pl.multiple_of(line * edge, edge), edge)
            left_high[target, at : at + edge] = high
            left_low[target, at : at + edge] = low
    dot = functools.partial(jnp.dot, preferred_element_type=jnp.float32)
    for m in range(0, CL, 2):
        columns = slice(m * edge, (m + 2) * edge)
        value = (
            dot(left_high[...], right_high[:, columns])
            + dot(left_low[...], right_high[:, columns])
            + dot(left_high[...], right_low[:, columns])
        )
        for l in range(RL):
            for k in range(2):
                at = l * CL + m + k
                piece = value[l * edge : (l + 1) * edge, k * edge : (k + 1) * edge]
                out_ref[at] = start_ref[at] + piece if has_start else piece


def product(narrow, change, crossing, table, shares, second, start=None):
    edge = second.shape[1]
    items = len(shares)
    choices = len(shares[0])
    slots = (shares[0][0].shape[0] - PAD) // edge
    depth = items * slots * edge
    scalars = pl.BlockSpec(memory_space=pltpu.SMEM)
    anywhere = pl.BlockSpec(memory_space=pl.ANY)
    whole = pl.BlockSpec(memory_space=pltpu.VMEM)
    starts = [] if start is None else [start]
    return pl.pallas_call(
        functools.partial(product_kernel, edge, slots, narrow, change, crossing, items, choices, start is not None),
        out_shape=jax.ShapeDtypeStruct((RL * CL, edge, edge), jnp.float32),
        in_specs=[scalars] + [anywhere] * (items * choices) + [whole] * (1 + len(starts)),
        out_specs=whole,
        scratch_shapes=[
            pltpu.VMEM((items, slots * edge, edge), jnp.float32),
            pltpu.SMEM((items, PAD, edge), jnp.float32),
            pltpu.VMEM((RL * edge, depth), jnp.bfloat16),
            pltpu.VMEM((RL * edge, depth), jnp.bfloat16),
            pltpu.VMEM((depth, CL * edge), jnp.bfloat16),
            pltpu.VMEM((depth, CL * edge), jnp.bfloat16),
            pltpu.SemaphoreType.DMA((items,)),
            pltpu.SemaphoreType.DMA((items,)),
        ],
        compiler_params=pltpu.CompilerParams(vmem_limit_bytes=VMEM_LIMIT),
        cost_estimate=pl.CostEstimate(
            flops=6 * RL * depth * CL * edge * edge, bytes_accessed=4 * 1024 * 1024, transcendentals=0
        ),
    )(table, *[ref for share in shares for ref in share], second, *starts)


def share_kernel(a_hbm, index_hbm, out_hbm, tile_ref, index_ref, block_sem, tile_sem, index_sem):
    slots, edge, _ = a_hbm.shape
    copies = [
        pltpu.make_async_copy(a_hbm.at[slot], out_hbm.at[pl.ds(slot * edge, edge)], block_sem.at[slot])
        for slot in range(slots)
    ]
    index_copy = pltpu.make_async_copy(index_hbm, index_ref, index_sem)
    index_copy.start()
    for copy in copies:
        copy.start()
    index_copy.wait()
    shape = tile_ref.shape
    row = lax.broadcasted_iota(jnp.int32, shape, 0)
    column = lax.broadcasted_iota(jnp.int32, shape, 1)
    tile = jnp.zeros(shape, jnp.float32)
    for n in range(2):
        for slot in range(slots):
            tile = jnp.where((row == n) & (column == slot), index_ref[0, n, slot].astype(jnp.float32), tile)
    tile_ref[...] = tile
    tile_copy = pltpu.make_async_copy(tile_ref, out_hbm.at[pl.ds(slots * edge, shape[0])], tile_sem)
    tile_copy.start()
    for copy in copies:
        copy.wait()
    tile_copy.wait()


def build_share(a_blocks, a_index):
    slots, edge, _ = a_blocks.shape
    return pl.pallas_call(
        share_kernel,
        out_shape=jax.ShapeDtypeStruct((slots * edge + PAD, edge), jnp.float32),
        in_specs=[pl.BlockSpec(memory_space=pl.ANY)] * 2,
        out_specs=pl.BlockSpec(memory_space=pl.ANY),
        scratch_shapes=[
            pltpu.VMEM((PAD, edge), jnp.float32),
            pltpu.SMEM(a_index.shape, jnp.int32),
            pltpu.SemaphoreType.DMA((slots,)),
            pltpu.SemaphoreType.DMA,
            pltpu.SemaphoreType.DMA,
        ],
        compiler_params=pltpu.CompilerParams(vmem_limit_bytes=1024 * 1024),
    )(pltpu.with_memory_space_constraint(a_blocks, pltpu.HBM), pltpu.with_memory_space_constraint(a_index, pltpu.HBM))


def block_table(b_index, narrow, wide):
    slots_second = b_index.shape[-1]
    table = jnp.arange((KBLOCKS // narrow + 1) * CL)[:, None]
    wanted = b_index[0, 0] // narrow * CL + b_index[0, 1] // wide
    hit = (table == wanted[None, :]) & (b_index[0, 0] >= 0)[None, :]
    found = jnp.where(hit, jnp.arange(slots_second)[None, :] - slots_second, 0)
    return (slots_second + jnp.sum(found, axis=1)).astype(jnp.int32)


def local(a_blocks, a_index, b_blocks, b_index):
    narrow = lax.axis_size("narrow")
    wide = lax.axis_size("wide")
    groups = narrow // 2
    planes = wide // 2
    slots = a_blocks.shape[1]
    edge = a_blocks.shape[-1]

    def permute(name, value, to):
        pairs = []
        for r in range(narrow):
            for c in range(wide):
                target = to(r, c)
                if target is not None:
                    pairs.append((c * narrow + r, target[1] * narrow + target[0]))
        with jax.named_scope(name):
            return lax.ppermute(value, AXES, pairs)

    def swap(name, value):
        return permute(name, value, lambda r, c: (r, c ^ 1))

    second = b_blocks[0]
    second_other = permute("second", second, lambda r, c: (r ^ 1, c))

    share = build_share(a_blocks[0], a_index)
    table = block_table(b_index, narrow, wide)
    tables = (table, permute("second_table", table, lambda r, c: (r ^ 1, c)))

    def spread(half, share, turn):
        def to(r, c):
            plane = c // 2
            u = plane % groups
            change = (r // 2) ^ u
            return (u * 2 + r % 2, (plane ^ change ^ turn) * 2 + c % 2)
        return permute(f"share_{half}_{turn}", share, to)

    far = permute("far", share, lambda r, c: (r, (c // 2 ^ groups) * 2 + c % 2))
    turns = [[spread(half, value, turn) for turn in range(groups)] for half, value in enumerate((share, far))]
    swapped = [[swap(f"swap_{half}", value) for value in values] for half, values in enumerate(turns)]
    candidates = [[ref for pair in zip(*values) for ref in pair] for values in zip(turns, swapped)]
    def window(change):
        value = product(narrow, change, 0, tables[0], candidates, second)
        return product(narrow, change, 1, tables[1], candidates, second_other, value)

    received = []
    for change in range(1, groups):
        value = window(change)
        received.append(permute(f"window_{change}", value, lambda r, c: (r ^ (change * 2), c)))
    total = window(0)
    for value in received:
        total = total + value
    return total.reshape(1, RL, 1, CL, edge, edge)


def solution(mesh):
    return jax.shard_map(
        local,
        mesh=mesh,
        in_specs=(
            P("narrow", "wide", None, None),
            P("narrow", None, "wide"),
            P("narrow", "wide", None, None),
            P("narrow", None, "wide"),
        ),
        out_specs=P("narrow", None, "wide", None, None, None),
        check_vma=False,
    )
```

```python
import functools

import jax
import jax.numpy as jnp
from jax import lax
from jax.experimental import pallas as pl
from jax.experimental.pallas import tpu as pltpu
from jax.sharding import PartitionSpec as P

RL = 2
CL = 4
KBLOCKS = 1024
PAD = 8
AXES = ("wide", "narrow")
VMEM_LIMIT = 20 * 1024 * 1024


def split(value):
    high = value.astype(jnp.bfloat16)
    low = (value - high.astype(jnp.float32)).astype(jnp.bfloat16)
    return high, low


def product_kernel(edge, slots, narrow, wide, change, choices, crossings, has_start, *refs):
    items = len(crossings)
    classes = sorted(set(crossings))
    empty_ref, refs = refs[0], refs[1:]
    shares = [refs[n * choices : (n + 1) * choices] for n in range(items)]
    refs = refs[items * choices :]
    second_refs, refs = dict(zip(classes, refs)), refs[len(classes) :]
    if has_start:
        start_ref, refs = refs[0], refs[1:]
    (out_ref, a_ref, index_ref, second_index, tables, left_high, left_low, right_high, right_low,
     block_sems, index_sems, second_sems, table_sems) = refs
    row, column = lax.axis_index("narrow"), lax.axis_index("wide")
    turn = (row // 2) ^ (column // 2 % (choices // 2)) ^ change
    rows = slots * edge
    slots_second = second_refs[classes[0]].shape[0] // edge
    table_copies = []
    for crossing in classes:
        tile = pl.ds(slots_second * edge, PAD)
        table_copies.append(
            pltpu.make_async_copy(second_refs[crossing].at[tile], second_index.at[crossing], second_sems.at[crossing])
        )
        table_copies.append(pltpu.make_async_copy(empty_ref, tables.at[crossing], table_sems.at[crossing]))

    def copies(n, ref):
        return (
            pltpu.make_async_copy(ref.at[pl.ds(rows, PAD)], index_ref.at[n], index_sems.at[n]),
            pltpu.make_async_copy(ref.at[pl.ds(0, rows)], a_ref.at[n], block_sems.at[n]),
        )

    for copy in table_copies:
        copy.start()
    for n, crossing in enumerate(crossings):
        pick = turn * 2 + ((row ^ column) % 2 ^ crossing)
        for choice in range(choices):
            @pl.when(pick == choice)
            def _():
                for copy in copies(n, shares[n][choice]):
                    copy.start()
    left_high[...] = jnp.zeros_like(left_high)
    left_low[...] = jnp.zeros_like(left_low)
    for copy in table_copies:
        copy.wait()
    for crossing in classes:
        for slot in range(slots_second):
            inner = second_index[crossing, 0, slot].astype(jnp.int32)
            outer = second_index[crossing, 1, slot].astype(jnp.int32)
            place = lax.div(jnp.maximum(inner, 0), narrow) * CL + lax.div(jnp.maximum(outer, 0), wide)
            tables[crossing, jnp.where(inner < 0, (KBLOCKS // narrow + 1) * CL, place)] = slot
    waits = [copies(n, shares[n][0]) for n in range(items)]
    for index_copy, _ in waits:
        index_copy.wait()
    for n, crossing in enumerate(crossings):
        for slot in range(slots):
            at = (n * slots + slot) * edge
            inner = index_ref[n, 1, slot].astype(jnp.int32)
            inner = jnp.where(inner < 0, KBLOCKS // narrow, lax.div(jnp.maximum(inner, 0), narrow))
            for m in range(CL):
                block = tables[crossing, inner * CL + m]
                source = pl.ds(pl.multiple_of(jnp.minimum(block, slots_second - 1) * edge, edge), edge)
                high, low = split(jnp.where(block < slots_second, second_refs[crossing][source, :], 0.0))
                right_high[at : at + edge, m * edge : (m + 1) * edge] = high
                right_low[at : at + edge, m * edge : (m + 1) * edge] = low
    for _, block_copy in waits:
        block_copy.wait()
    for n in range(items):
        for slot in range(slots):
            at = (n * slots + slot) * edge
            line = lax.div(jnp.maximum(index_ref[n, 0, slot].astype(jnp.int32), 0), narrow)
            high, low = split(a_ref[n, slot * edge : (slot + 1) * edge, :])
            target = pl.ds(pl.multiple_of(line * edge, edge), edge)
            left_high[target, at : at + edge] = high
            left_low[target, at : at + edge] = low
    dot = functools.partial(jnp.dot, preferred_element_type=jnp.float32)
    for m in range(0, CL, 2):
        columns = slice(m * edge, (m + 2) * edge)
        value = (
            dot(left_high[...], right_high[:, columns])
            + dot(left_low[...], right_high[:, columns])
            + dot(left_high[...], right_low[:, columns])
        )
        for l in range(RL):
            for k in range(2):
                at = l * CL + m + k
                piece = value[l * edge : (l + 1) * edge, k * edge : (k + 1) * edge]
                out_ref[at] = start_ref[at] + piece if has_start else piece


def product(narrow, wide, change, crossings, shares, seconds, start=None):
    edge = shares[0][0].shape[1]
    items = len(shares)
    choices = len(shares[0])
    slots = (shares[0][0].shape[0] - PAD) // edge
    depth = items * slots * edge
    anywhere = pl.BlockSpec(memory_space=pl.ANY)
    whole = pl.BlockSpec(memory_space=pltpu.VMEM)
    places = (KBLOCKS // narrow + 2) * CL
    empty = jnp.full((places,), seconds[0].shape[0] // edge, jnp.int32)
    operands = [seconds[crossing] for crossing in sorted(set(crossings))]
    if start is not None:
        operands.append(start)
    return pl.pallas_call(
        functools.partial(product_kernel, edge, slots, narrow, wide, change, choices, crossings, start is not None),
        out_shape=jax.ShapeDtypeStruct((RL * CL, edge, edge), jnp.float32),
        in_specs=[anywhere] * (1 + items * choices) + [whole] * len(operands),
        out_specs=whole,
        scratch_shapes=[
            pltpu.VMEM((items, slots * edge, edge), jnp.float32),
            pltpu.SMEM((items, PAD, edge), jnp.float32),
            pltpu.SMEM((2, PAD, edge), jnp.float32),
            pltpu.SMEM((2, places), jnp.int32),
            pltpu.VMEM((RL * edge, depth), jnp.bfloat16),
            pltpu.VMEM((RL * edge, depth), jnp.bfloat16),
            pltpu.VMEM((depth, CL * edge), jnp.bfloat16),
            pltpu.VMEM((depth, CL * edge), jnp.bfloat16),
            pltpu.SemaphoreType.DMA((items,)),
            pltpu.SemaphoreType.DMA((items,)),
            pltpu.SemaphoreType.DMA((2,)),
            pltpu.SemaphoreType.DMA((2,)),
        ],
        compiler_params=pltpu.CompilerParams(vmem_limit_bytes=VMEM_LIMIT),
        cost_estimate=pl.CostEstimate(
            flops=6 * RL * depth * CL * edge * edge, bytes_accessed=4 * 1024 * 1024, transcendentals=0
        ),
    )(empty, *[ref for share in shares for ref in share], *operands)


def share_kernel(*refs):
    arrays = len(refs) // 7
    parts = [refs[n * arrays : (n + 1) * arrays] for n in range(7)]
    waits = []
    for blocks_hbm, index_hbm, out_hbm, tile_ref, index_ref, block_sem, index_sem in zip(*parts):
        slots, edge, _ = blocks_hbm.shape
        copies = [
            pltpu.make_async_copy(blocks_hbm.at[slot], out_hbm.at[pl.ds(slot * edge, edge)], block_sem.at[slot])
            for slot in range(slots)
        ]
        index_copy = pltpu.make_async_copy(index_hbm, index_ref, index_sem)
        index_copy.start()
        for copy in copies:
            copy.start()
        waits += copies
    for blocks_hbm, index_hbm, out_hbm, tile_ref, index_ref, block_sem, index_sem in zip(*parts):
        slots, edge, _ = blocks_hbm.shape
        pltpu.make_async_copy(index_hbm, index_ref, index_sem).wait()
        shape = tile_ref.shape
        row = lax.broadcasted_iota(jnp.int32, shape, 0)
        column = lax.broadcasted_iota(jnp.int32, shape, 1)
        tile = jnp.zeros(shape, jnp.float32)
        for n in range(2):
            for slot in range(slots):
                tile = jnp.where((row == n) & (column == slot), index_ref[0, n, slot].astype(jnp.float32), tile)
        tile_ref[...] = tile
        tile_copy = pltpu.make_async_copy(tile_ref, out_hbm.at[pl.ds(slots * edge, PAD)], block_sem.at[slots])
        tile_copy.start()
        waits.append(tile_copy)
    for copy in waits:
        copy.wait()


def build_shares(blocks, indices):
    anywhere = pl.BlockSpec(memory_space=pl.ANY)
    return pl.pallas_call(
        share_kernel,
        out_shape=tuple(
            jax.ShapeDtypeStruct((value.shape[0] * value.shape[1] + PAD, value.shape[2]), jnp.float32) for value in blocks
        ),
        in_specs=[anywhere] * (2 * len(blocks)),
        out_specs=(anywhere,) * len(blocks),
        scratch_shapes=[pltpu.VMEM((PAD, value.shape[2]), jnp.float32) for value in blocks]
        + [pltpu.SMEM(value.shape, jnp.int32) for value in indices]
        + [pltpu.SemaphoreType.DMA((value.shape[0] + 1,)) for value in blocks]
        + [pltpu.SemaphoreType.DMA for _ in blocks],
        compiler_params=pltpu.CompilerParams(vmem_limit_bytes=1024 * 1024),
    )(*[pltpu.with_memory_space_constraint(value, pltpu.HBM) for value in (*blocks, *indices)])


def local(a_blocks, a_index, b_blocks, b_index):
    narrow = lax.axis_size("narrow")
    wide = lax.axis_size("wide")
    groups = narrow // 2
    planes = wide // 2
    slots = a_blocks.shape[1]
    edge = a_blocks.shape[-1]

    def permute(name, value, to):
        pairs = []
        for r in range(narrow):
            for c in range(wide):
                target = to(r, c)
                if target is not None:
                    pairs.append((c * narrow + r, target[1] * narrow + target[0]))
        with jax.named_scope(name):
            return lax.ppermute(value, AXES, pairs)

    def swap(name, value):
        return permute(name, value, lambda r, c: (r, c ^ 1))

    share, second = build_shares((a_blocks[0], b_blocks[0]), (a_index, b_index))
    second_other = permute("second", second, lambda r, c: (r ^ 1, c))

    def spread(half, share, turn):
        def to(r, c):
            plane = c // 2
            u = plane % groups
            change = (r // 2) ^ u
            return (u * 2 + r % 2, (plane ^ change ^ turn) * 2 + c % 2)
        return permute(f"share_{half}_{turn}", share, to)

    far = permute("far", share, lambda r, c: (r, (c // 2 ^ groups) * 2 + c % 2))
    turns = [[spread(half, value, turn) for turn in range(groups)] for half, value in enumerate((share, far))]
    swapped = [[swap(f"swap_{half}", value) for value in values] for half, values in enumerate(turns)]
    candidates = [[ref for pair in zip(*values) for ref in pair] for values in zip(turns, swapped)]
    seconds = (second, second_other)
    received = []
    for change in range(1, groups):
        value = product(narrow, wide, change, (0, 0, 1, 1), candidates * 2, seconds)
        received.append(permute(f"window_{change}", value, lambda r, c: (r ^ (change * 2), c)))
    total = product(narrow, wide, 0, (0, 0), candidates, seconds)
    total = product(narrow, wide, 0, (1, 1), candidates, seconds, total)
    for value in received:
        total = total + value
    return total.reshape(1, RL, 1, CL, edge, edge)


def solution(mesh):
    return jax.shard_map(
        local,
        mesh=mesh,
        in_specs=(
            P("narrow", "wide", None, None),
            P("narrow", None, "wide"),
            P("narrow", "wide", None, None),
            P("narrow", None, "wide"),
        ),
        out_specs=P("narrow", None, "wide", None, None, None),
        check_vma=False,
    )
```

```python
import functools

import jax
import jax.numpy as jnp
from jax import lax
from jax.experimental import pallas as pl
from jax.experimental.pallas import tpu as pltpu
from jax.sharding import PartitionSpec as P

RL = 2
CL = 4
KBLOCKS = 1024
PAD = 8
AXES = ("wide", "narrow")
VMEM_LIMIT = 20 * 1024 * 1024


def split(value):
    high = value.astype(jnp.bfloat16)
    low = (value - high.astype(jnp.float32)).astype(jnp.bfloat16)
    return high, low


def product_kernel(edge, slots, narrow, wide, change, choices, crossings, has_start, *refs):
    items = len(crossings)
    classes = sorted(set(crossings))
    empty_ref, refs = refs[0], refs[1:]
    shares = [refs[n * choices : (n + 1) * choices] for n in range(items)]
    refs = refs[items * choices :]
    second_refs, refs = dict(zip(classes, refs)), refs[len(classes) :]
    if has_start:
        start_ref, refs = refs[0], refs[1:]
    (out_ref, a_ref, index_ref, second_index, tables, left_high, left_low, right_high, right_low,
     block_sems, index_sems, second_sems, table_sems) = refs
    row, column = lax.axis_index("narrow"), lax.axis_index("wide")
    turn = (row // 2) ^ (column // 2 % (choices // 2)) ^ change
    rows = slots * edge
    slots_second = second_refs[classes[0]].shape[0] // edge
    table_copies = []
    for crossing in classes:
        tile = pl.ds(slots_second * edge, PAD)
        table_copies.append(
            pltpu.make_async_copy(second_refs[crossing].at[tile], second_index.at[crossing], second_sems.at[crossing])
        )
        table_copies.append(pltpu.make_async_copy(empty_ref, tables.at[crossing], table_sems.at[crossing]))

    def copies(n, ref):
        return (
            pltpu.make_async_copy(ref.at[pl.ds(rows, PAD)], index_ref.at[n], index_sems.at[n]),
            pltpu.make_async_copy(ref.at[pl.ds(0, rows)], a_ref.at[n], block_sems.at[n]),
        )

    for copy in table_copies:
        copy.start()
    for n, crossing in enumerate(crossings):
        pick = turn * 2 + ((row ^ column) % 2 ^ crossing)
        for choice in range(choices):
            @pl.when(pick == choice)
            def _():
                for copy in copies(n, shares[n][choice]):
                    copy.start()
    left_high[...] = jnp.zeros_like(left_high)
    left_low[...] = jnp.zeros_like(left_low)
    for copy in table_copies:
        copy.wait()
    for crossing in classes:
        for slot in range(slots_second):
            inner = second_index[crossing, 0, slot].astype(jnp.int32)
            outer = second_index[crossing, 1, slot].astype(jnp.int32)
            place = lax.div(jnp.maximum(inner, 0), narrow) * CL + lax.div(jnp.maximum(outer, 0), wide)
            tables[crossing, jnp.where(inner < 0, (KBLOCKS // narrow + 1) * CL, place)] = slot
    waits = [copies(n, shares[n][0]) for n in range(items)]
    for index_copy, _ in waits:
        index_copy.wait()
    for n, crossing in enumerate(crossings):
        for slot in range(slots):
            at = (n * slots + slot) * edge
            inner = index_ref[n, 1, slot].astype(jnp.int32)
            inner = jnp.where(inner < 0, KBLOCKS // narrow, lax.div(jnp.maximum(inner, 0), narrow))
            for m in range(CL):
                block = tables[crossing, inner * CL + m]
                source = pl.ds(pl.multiple_of(jnp.minimum(block, slots_second - 1) * edge, edge), edge)
                high, low = split(jnp.where(block < slots_second, second_refs[crossing][source, :], 0.0))
                right_high[at : at + edge, m * edge : (m + 1) * edge] = high
                right_low[at : at + edge, m * edge : (m + 1) * edge] = low
    for _, block_copy in waits:
        block_copy.wait()
    for n in range(items):
        for slot in range(slots):
            at = (n * slots + slot) * edge
            line = lax.div(jnp.maximum(index_ref[n, 0, slot].astype(jnp.int32), 0), narrow)
            high, low = split(a_ref[n, slot * edge : (slot + 1) * edge, :])
            target = pl.ds(pl.multiple_of(line * edge, edge), edge)
            left_high[target, at : at + edge] = high
            left_low[target, at : at + edge] = low
    dot = functools.partial(jnp.dot, preferred_element_type=jnp.float32)
    for m in range(0, CL, 2):
        columns = slice(m * edge, (m + 2) * edge)
        value = (
            dot(left_high[...], right_high[:, columns])
            + dot(left_low[...], right_high[:, columns])
            + dot(left_high[...], right_low[:, columns])
        )
        for l in range(RL):
            for k in range(2):
                at = l * CL + m + k
                piece = value[l * edge : (l + 1) * edge, k * edge : (k + 1) * edge]
                out_ref[at] = start_ref[at] + piece if has_start else piece


def product(narrow, wide, change, crossings, shares, seconds, start=None):
    edge = shares[0][0].shape[1]
    items = len(shares)
    choices = len(shares[0])
    slots = (shares[0][0].shape[0] - PAD) // edge
    depth = items * slots * edge
    anywhere = pl.BlockSpec(memory_space=pl.ANY)
    whole = pl.BlockSpec(memory_space=pltpu.VMEM)
    places = (KBLOCKS // narrow + 2) * CL
    empty = jnp.full((places,), seconds[0].shape[0] // edge, jnp.int32)
    operands = [seconds[crossing] for crossing in sorted(set(crossings))]
    if start is not None:
        operands.append(start)
    return pl.pallas_call(
        functools.partial(product_kernel, edge, slots, narrow, wide, change, choices, crossings, start is not None),
        out_shape=jax.ShapeDtypeStruct((RL * CL, edge, edge), jnp.float32),
        in_specs=[anywhere] * (1 + items * choices) + [whole] * len(operands),
        out_specs=whole,
        scratch_shapes=[
            pltpu.VMEM((items, slots * edge, edge), jnp.float32),
            pltpu.SMEM((items, PAD, edge), jnp.float32),
            pltpu.SMEM((2, PAD, edge), jnp.float32),
            pltpu.SMEM((2, places), jnp.int32),
            pltpu.VMEM((RL * edge, depth), jnp.bfloat16),
            pltpu.VMEM((RL * edge, depth), jnp.bfloat16),
            pltpu.VMEM((depth, CL * edge), jnp.bfloat16),
            pltpu.VMEM((depth, CL * edge), jnp.bfloat16),
            pltpu.SemaphoreType.DMA((items,)),
            pltpu.SemaphoreType.DMA((items,)),
            pltpu.SemaphoreType.DMA((2,)),
            pltpu.SemaphoreType.DMA((2,)),
        ],
        compiler_params=pltpu.CompilerParams(vmem_limit_bytes=VMEM_LIMIT),
        cost_estimate=pl.CostEstimate(
            flops=6 * RL * depth * CL * edge * edge, bytes_accessed=4 * 1024 * 1024, transcendentals=0
        ),
    )(empty, *[ref for share in shares for ref in share], *operands)


def share_kernel(*refs):
    arrays = len(refs) // 7
    parts = [refs[n * arrays : (n + 1) * arrays] for n in range(7)]
    waits = []
    for blocks_hbm, index_hbm, out_hbm, tile_ref, index_ref, block_sem, index_sem in zip(*parts):
        slots, edge, _ = blocks_hbm.shape
        copies = [
            pltpu.make_async_copy(blocks_hbm.at[slot], out_hbm.at[pl.ds(slot * edge, edge)], block_sem.at[slot])
            for slot in range(slots)
        ]
        index_copy = pltpu.make_async_copy(index_hbm, index_ref, index_sem)
        index_copy.start()
        for copy in copies:
            copy.start()
        waits += copies
    for blocks_hbm, index_hbm, out_hbm, tile_ref, index_ref, block_sem, index_sem in zip(*parts):
        slots, edge, _ = blocks_hbm.shape
        pltpu.make_async_copy(index_hbm, index_ref, index_sem).wait()
        shape = tile_ref.shape
        row = lax.broadcasted_iota(jnp.int32, shape, 0)
        column = lax.broadcasted_iota(jnp.int32, shape, 1)
        tile = jnp.zeros(shape, jnp.float32)
        for n in range(2):
            for slot in range(slots):
                tile = jnp.where((row == n) & (column == slot), index_ref[0, n, slot].astype(jnp.float32), tile)
        tile_ref[...] = tile
        tile_copy = pltpu.make_async_copy(tile_ref, out_hbm.at[pl.ds(slots * edge, PAD)], block_sem.at[slots])
        tile_copy.start()
        waits.append(tile_copy)
    for copy in waits:
        copy.wait()


def build_shares(blocks, indices):
    anywhere = pl.BlockSpec(memory_space=pl.ANY)
    return pl.pallas_call(
        share_kernel,
        out_shape=tuple(
            jax.ShapeDtypeStruct((value.shape[0] * value.shape[1] + PAD, value.shape[2]), jnp.float32) for value in blocks
        ),
        in_specs=[anywhere] * (2 * len(blocks)),
        out_specs=(anywhere,) * len(blocks),
        scratch_shapes=[pltpu.VMEM((PAD, value.shape[2]), jnp.float32) for value in blocks]
        + [pltpu.SMEM(value.shape, jnp.int32) for value in indices]
        + [pltpu.SemaphoreType.DMA((value.shape[0] + 1,)) for value in blocks]
        + [pltpu.SemaphoreType.DMA for _ in blocks],
        compiler_params=pltpu.CompilerParams(vmem_limit_bytes=1024 * 1024),
    )(*[pltpu.with_memory_space_constraint(value, pltpu.HBM) for value in (*blocks, *indices)])


def local(a_blocks, a_index, b_blocks, b_index):
    narrow = lax.axis_size("narrow")
    wide = lax.axis_size("wide")
    groups = narrow // 2
    planes = wide // 2
    slots = a_blocks.shape[1]
    edge = a_blocks.shape[-1]

    def permute(name, value, to):
        pairs = []
        for r in range(narrow):
            for c in range(wide):
                target = to(r, c)
                if target is not None:
                    pairs.append((c * narrow + r, target[1] * narrow + target[0]))
        with jax.named_scope(name):
            return lax.ppermute(value, AXES, pairs)

    def swap(name, value):
        return permute(name, value, lambda r, c: (r, c ^ 1))

    share, second = build_shares((a_blocks[0], b_blocks[0]), (a_index, b_index))
    second_other = permute("second", second, lambda r, c: (r ^ 1, c))

    def spread(half, share, turn):
        def to(r, c):
            plane = c // 2
            u = plane % groups
            change = (r // 2) ^ u
            return (u * 2 + r % 2, (plane ^ change ^ turn) * 2 + c % 2)
        return permute(f"share_{half}_{turn}", share, to)

    far = permute("far", share, lambda r, c: (r, (c // 2 ^ groups) * 2 + c % 2))
    turns = [[spread(half, value, turn) for turn in range(groups)] for half, value in enumerate((share, far))]
    swapped = [[swap(f"swap_{half}", value) for value in values] for half, values in enumerate(turns)]
    candidates = [[ref for pair in zip(*values) for ref in pair] for values in zip(turns, swapped)]
    seconds = (second, second_other)
    received = []
    for change in range(1, groups):
        value = product(narrow, wide, change, (0,), candidates[:1], seconds)
        value = product(narrow, wide, change, (0, 1, 1), [candidates[1], *candidates], seconds, value)
        received.append(permute(f"window_{change}", value, lambda r, c: (r ^ (change * 2), c)))
    total = product(narrow, wide, 0, (0, 0), candidates, seconds)
    total = product(narrow, wide, 0, (1, 1), candidates, seconds, total)
    for value in received:
        total = total + value
    return total.reshape(1, RL, 1, CL, edge, edge)


def solution(mesh):
    return jax.shard_map(
        local,
        mesh=mesh,
        in_specs=(
            P("narrow", "wide", None, None),
            P("narrow", None, "wide"),
            P("narrow", "wide", None, None),
            P("narrow", None, "wide"),
        ),
        out_specs=P("narrow", None, "wide", None, None, None),
        check_vma=False,
    )
```

```python
import functools

import jax
import jax.numpy as jnp
from jax import lax
from jax.experimental import pallas as pl
from jax.experimental.pallas import tpu as pltpu
from jax.sharding import PartitionSpec as P

RL = 2
CL = 4
KBLOCKS = 1024
PAD = 8
AXES = ("wide", "narrow")
VMEM_LIMIT = 20 * 1024 * 1024


def split(value):
    high = value.astype(jnp.bfloat16)
    low = (value - high.astype(jnp.float32)).astype(jnp.bfloat16)
    return high, low


def product_kernel(edge, slots, narrow, wide, change, choices, crossings, outer, has_start, *refs):
    width = len(outer)
    items = len(crossings)
    classes = sorted(set(crossings))
    empty_ref, refs = refs[0], refs[1:]
    shares = [refs[n * choices : (n + 1) * choices] for n in range(items)]
    refs = refs[items * choices :]
    second_refs, refs = dict(zip(classes, refs)), refs[len(classes) :]
    if has_start:
        start_ref, refs = refs[0], refs[1:]
    (out_ref, a_ref, index_ref, second_index, tables, left_high, left_low, right_high, right_low,
     block_sems, index_sems, second_sems, table_sems) = refs
    row, column = lax.axis_index("narrow"), lax.axis_index("wide")
    turn = (row // 2) ^ (column // 2 % (choices // 2)) ^ change
    rows = slots * edge
    slots_second = second_refs[classes[0]].shape[0] // edge
    table_copies = []
    for crossing in classes:
        tile = pl.ds(slots_second * edge, PAD)
        table_copies.append(
            pltpu.make_async_copy(second_refs[crossing].at[tile], second_index.at[crossing], second_sems.at[crossing])
        )
        table_copies.append(pltpu.make_async_copy(empty_ref, tables.at[crossing], table_sems.at[crossing]))

    def copies(n, ref):
        return (
            pltpu.make_async_copy(ref.at[pl.ds(rows, PAD)], index_ref.at[n], index_sems.at[n]),
            pltpu.make_async_copy(ref.at[pl.ds(0, rows)], a_ref.at[n], block_sems.at[n]),
        )

    for copy in table_copies:
        copy.start()
    for n, crossing in enumerate(crossings):
        pick = turn * 2 + ((row ^ column) % 2 ^ crossing)
        for choice in range(choices):
            @pl.when(pick == choice)
            def _():
                for copy in copies(n, shares[n][choice]):
                    copy.start()
    left_high[...] = jnp.zeros_like(left_high)
    left_low[...] = jnp.zeros_like(left_low)
    for copy in table_copies:
        copy.wait()
    for crossing in classes:
        for slot in range(slots_second):
            inner = second_index[crossing, 0, slot].astype(jnp.int32)
            across = second_index[crossing, 1, slot].astype(jnp.int32)
            place = lax.div(jnp.maximum(inner, 0), narrow) * CL + lax.div(jnp.maximum(across, 0), wide)
            tables[crossing, jnp.where(inner < 0, (KBLOCKS // narrow + 1) * CL, place)] = slot
    waits = [copies(n, shares[n][0]) for n in range(items)]
    for index_copy, _ in waits:
        index_copy.wait()
    for _, block_copy in waits:
        block_copy.wait()
    for n, crossing in enumerate(crossings):
        for slot in range(slots):
            at = (n * slots + slot) * edge
            inner = index_ref[n, 1, slot].astype(jnp.int32)
            inner = jnp.where(inner < 0, KBLOCKS // narrow, lax.div(jnp.maximum(inner, 0), narrow))
            for at_column, m in enumerate(outer):
                block = tables[crossing, inner * CL + m]
                source = pl.ds(pl.multiple_of(jnp.minimum(block, slots_second - 1) * edge, edge), edge)
                high, low = split(jnp.where(block < slots_second, second_refs[crossing][source, :], 0.0))
                right_high[at : at + edge, at_column * edge : (at_column + 1) * edge] = high
                right_low[at : at + edge, at_column * edge : (at_column + 1) * edge] = low
    for n in range(items):
        for slot in range(slots):
            at = (n * slots + slot) * edge
            line = lax.div(jnp.maximum(index_ref[n, 0, slot].astype(jnp.int32), 0), narrow)
            high, low = split(a_ref[n, slot * edge : (slot + 1) * edge, :])
            target = pl.ds(pl.multiple_of(line * edge, edge), edge)
            left_high[target, at : at + edge] = high
            left_low[target, at : at + edge] = low
    dot = functools.partial(jnp.dot, preferred_element_type=jnp.float32)
    for m in range(0, width, 2):
        columns = slice(m * edge, (m + 2) * edge)
        value = (
            dot(left_high[...], right_high[:, columns])
            + dot(left_low[...], right_high[:, columns])
            + dot(left_high[...], right_low[:, columns])
        )
        for l in range(RL):
            for k in range(2):
                at = l * width + m + k
                piece = value[l * edge : (l + 1) * edge, k * edge : (k + 1) * edge]
                out_ref[at] = start_ref[l * CL + outer[m + k]] + piece if has_start else piece


def product(narrow, wide, change, crossings, shares, seconds, start=None, outer=tuple(range(CL))):
    edge = shares[0][0].shape[1]
    items = len(shares)
    choices = len(shares[0])
    slots = (shares[0][0].shape[0] - PAD) // edge
    depth = items * slots * edge
    anywhere = pl.BlockSpec(memory_space=pl.ANY)
    whole = pl.BlockSpec(memory_space=pltpu.VMEM)
    places = (KBLOCKS // narrow + 2) * CL
    empty = jnp.full((places,), seconds[0].shape[0] // edge, jnp.int32)
    operands = [seconds[crossing] for crossing in sorted(set(crossings))]
    if start is not None:
        operands.append(start)
    return pl.pallas_call(
        functools.partial(product_kernel, edge, slots, narrow, wide, change, choices, crossings, outer, start is not None),
        out_shape=jax.ShapeDtypeStruct((RL * len(outer), edge, edge), jnp.float32),
        in_specs=[anywhere] * (1 + items * choices) + [whole] * len(operands),
        out_specs=whole,
        scratch_shapes=[
            pltpu.VMEM((items, slots * edge, edge), jnp.float32),
            pltpu.SMEM((items, PAD, edge), jnp.float32),
            pltpu.SMEM((2, PAD, edge), jnp.float32),
            pltpu.SMEM((2, places), jnp.int32),
            pltpu.VMEM((RL * edge, depth), jnp.bfloat16),
            pltpu.VMEM((RL * edge, depth), jnp.bfloat16),
            pltpu.VMEM((depth, len(outer) * edge), jnp.bfloat16),
            pltpu.VMEM((depth, len(outer) * edge), jnp.bfloat16),
            pltpu.SemaphoreType.DMA((items,)),
            pltpu.SemaphoreType.DMA((items,)),
            pltpu.SemaphoreType.DMA((2,)),
            pltpu.SemaphoreType.DMA((2,)),
        ],
        compiler_params=pltpu.CompilerParams(vmem_limit_bytes=VMEM_LIMIT),
        cost_estimate=pl.CostEstimate(
            flops=6 * RL * depth * len(outer) * edge * edge, bytes_accessed=4 * 1024 * 1024, transcendentals=0
        ),
    )(empty, *[ref for share in shares for ref in share], *operands)


def share_kernel(*refs):
    arrays = len(refs) // 7
    parts = [refs[n * arrays : (n + 1) * arrays] for n in range(7)]
    waits = []
    for blocks_hbm, index_hbm, out_hbm, tile_ref, index_ref, block_sem, index_sem in zip(*parts):
        slots, edge, _ = blocks_hbm.shape
        copies = [
            pltpu.make_async_copy(blocks_hbm.at[slot], out_hbm.at[pl.ds(slot * edge, edge)], block_sem.at[slot])
            for slot in range(slots)
        ]
        index_copy = pltpu.make_async_copy(index_hbm, index_ref, index_sem)
        index_copy.start()
        for copy in copies:
            copy.start()
        waits += copies
    for blocks_hbm, index_hbm, out_hbm, tile_ref, index_ref, block_sem, index_sem in zip(*parts):
        slots, edge, _ = blocks_hbm.shape
        pltpu.make_async_copy(index_hbm, index_ref, index_sem).wait()
        shape = tile_ref.shape
        row = lax.broadcasted_iota(jnp.int32, shape, 0)
        column = lax.broadcasted_iota(jnp.int32, shape, 1)
        tile = jnp.zeros(shape, jnp.float32)
        for n in range(2):
            for slot in range(slots):
                tile = jnp.where((row == n) & (column == slot), index_ref[0, n, slot].astype(jnp.float32), tile)
        tile_ref[...] = tile
        tile_copy = pltpu.make_async_copy(tile_ref, out_hbm.at[pl.ds(slots * edge, PAD)], block_sem.at[slots])
        tile_copy.start()
        waits.append(tile_copy)
    for copy in waits:
        copy.wait()


def build_shares(blocks, indices):
    anywhere = pl.BlockSpec(memory_space=pl.ANY)
    return pl.pallas_call(
        share_kernel,
        out_shape=tuple(
            jax.ShapeDtypeStruct((value.shape[0] * value.shape[1] + PAD, value.shape[2]), jnp.float32) for value in blocks
        ),
        in_specs=[anywhere] * (2 * len(blocks)),
        out_specs=(anywhere,) * len(blocks),
        scratch_shapes=[pltpu.VMEM((PAD, value.shape[2]), jnp.float32) for value in blocks]
        + [pltpu.SMEM(value.shape, jnp.int32) for value in indices]
        + [pltpu.SemaphoreType.DMA((value.shape[0] + 1,)) for value in blocks]
        + [pltpu.SemaphoreType.DMA for _ in blocks],
        compiler_params=pltpu.CompilerParams(vmem_limit_bytes=1024 * 1024),
    )(*[pltpu.with_memory_space_constraint(value, pltpu.HBM) for value in (*blocks, *indices)])


def local(a_blocks, a_index, b_blocks, b_index):
    narrow = lax.axis_size("narrow")
    wide = lax.axis_size("wide")
    groups = narrow // 2
    planes = wide // 2
    slots = a_blocks.shape[1]
    edge = a_blocks.shape[-1]

    def permute(name, value, to):
        pairs = []
        for r in range(narrow):
            for c in range(wide):
                target = to(r, c)
                if target is not None:
                    pairs.append((c * narrow + r, target[1] * narrow + target[0]))
        with jax.named_scope(name):
            return lax.ppermute(value, AXES, pairs)

    def swap(name, value):
        return permute(name, value, lambda r, c: (r, c ^ 1))

    share, second = build_shares((a_blocks[0], b_blocks[0]), (a_index, b_index))
    second_other = permute("second", second, lambda r, c: (r ^ 1, c))

    def spread(half, share, turn):
        def to(r, c):
            plane = c // 2
            u = plane % groups
            change = (r // 2) ^ u
            return (u * 2 + r % 2, (plane ^ change ^ turn) * 2 + c % 2)
        return permute(f"share_{half}_{turn}", share, to)

    far = permute("far", share, lambda r, c: (r, (c // 2 ^ groups) * 2 + c % 2))
    turns = [[spread(half, value, turn) for turn in range(groups)] for half, value in enumerate((share, far))]
    swapped = [[swap(f"swap_{half}", value) for value in values] for half, values in enumerate(turns)]
    candidates = [[ref for pair in zip(*values) for ref in pair] for values in zip(turns, swapped)]
    seconds = (second, second_other)
    received = []
    for change in range(1, groups):
        start = product(narrow, wide, change, (0,), candidates[:1], seconds)
        pieces = []
        for outer in (tuple(range(CL // 2)), tuple(range(CL // 2, CL))):
            value = product(narrow, wide, change, (0, 1, 1), [candidates[1], *candidates], seconds, start, outer)
            got = permute(f"window_{change}", value, lambda r, c: (r ^ (change * 2), c))
            pieces.append(got.reshape(RL, len(outer), edge, edge))
        received.append(jnp.concatenate(pieces, axis=1))
    total = product(narrow, wide, 0, (0, 0), candidates, seconds)
    total = product(narrow, wide, 0, (1, 1), candidates, seconds, total).reshape(RL, CL, edge, edge)
    for value in received:
        total = total + value
    return total.reshape(1, RL, 1, CL, edge, edge)


def solution(mesh):
    return jax.shard_map(
        local,
        mesh=mesh,
        in_specs=(
            P("narrow", "wide", None, None),
            P("narrow", None, "wide"),
            P("narrow", "wide", None, None),
            P("narrow", None, "wide"),
        ),
        out_specs=P("narrow", None, "wide", None, None, None),
        check_vma=False,
    )
```

```python
import functools

import jax
import jax.numpy as jnp
from jax import lax
from jax.experimental import pallas as pl
from jax.experimental.pallas import tpu as pltpu
from jax.sharding import PartitionSpec as P

RL = 2
CL = 4
KBLOCKS = 1024
PAD = 8
AXES = ("wide", "narrow")
VMEM_LIMIT = 20 * 1024 * 1024


def split(value):
    high = value.astype(jnp.bfloat16)
    low = (value - high.astype(jnp.float32)).astype(jnp.bfloat16)
    return high, low


def product_kernel(edge, slots, narrow, wide, change, choices, crossings, outer, has_start, afters, *refs):
    width = len(outer)
    items = len(crossings)
    classes = sorted(set(crossings))
    empty_ref, refs = refs[afters], refs[afters + 1 :]
    shares = [refs[n * choices : (n + 1) * choices] for n in range(items)]
    refs = refs[items * choices :]
    second_refs, refs = dict(zip(classes, refs)), refs[len(classes) :]
    if has_start:
        start_ref, refs = refs[0], refs[1:]
    (out_ref, a_ref, index_ref, second_index, tables, left_high, left_low, right_high, right_low,
     block_sems, index_sems, second_sems, table_sems) = refs
    row, column = lax.axis_index("narrow"), lax.axis_index("wide")
    turn = (row // 2) ^ (column // 2 % (choices // 2)) ^ change
    rows = slots * edge
    slots_second = second_refs[classes[0]].shape[0] // edge
    table_copies = []
    for crossing in classes:
        tile = pl.ds(slots_second * edge, PAD)
        table_copies.append(
            pltpu.make_async_copy(second_refs[crossing].at[tile], second_index.at[crossing], second_sems.at[crossing])
        )
        table_copies.append(pltpu.make_async_copy(empty_ref, tables.at[crossing], table_sems.at[crossing]))

    def copies(n, ref):
        return (
            pltpu.make_async_copy(ref.at[pl.ds(rows, PAD)], index_ref.at[n], index_sems.at[n]),
            pltpu.make_async_copy(ref.at[pl.ds(0, rows)], a_ref.at[n], block_sems.at[n]),
        )

    for copy in table_copies:
        copy.start()
    for n, crossing in enumerate(crossings):
        pick = turn * 2 + ((row ^ column) % 2 ^ crossing)
        for choice in range(choices):
            @pl.when(pick == choice)
            def _():
                for copy in copies(n, shares[n][choice]):
                    copy.start()
    left_high[...] = jnp.zeros_like(left_high)
    left_low[...] = jnp.zeros_like(left_low)
    for copy in table_copies:
        copy.wait()
    for crossing in classes:
        for slot in range(slots_second):
            inner = second_index[crossing, 0, slot].astype(jnp.int32)
            across = second_index[crossing, 1, slot].astype(jnp.int32)
            place = lax.div(jnp.maximum(inner, 0), narrow) * CL + lax.div(jnp.maximum(across, 0), wide)
            tables[crossing, jnp.where(inner < 0, (KBLOCKS // narrow + 1) * CL, place)] = slot
    waits = [copies(n, shares[n][0]) for n in range(items)]
    for index_copy, _ in waits:
        index_copy.wait()
    for _, block_copy in waits:
        block_copy.wait()
    for n, crossing in enumerate(crossings):
        for slot in range(slots):
            at = (n * slots + slot) * edge
            inner = index_ref[n, 1, slot].astype(jnp.int32)
            inner = jnp.where(inner < 0, KBLOCKS // narrow, lax.div(jnp.maximum(inner, 0), narrow))
            for at_column, m in enumerate(outer):
                block = tables[crossing, inner * CL + m]
                source = pl.ds(pl.multiple_of(jnp.minimum(block, slots_second - 1) * edge, edge), edge)
                high, low = split(jnp.where(block < slots_second, second_refs[crossing][source, :], 0.0))
                right_high[at : at + edge, at_column * edge : (at_column + 1) * edge] = high
                right_low[at : at + edge, at_column * edge : (at_column + 1) * edge] = low
    for n in range(items):
        for slot in range(slots):
            at = (n * slots + slot) * edge
            line = lax.div(jnp.maximum(index_ref[n, 0, slot].astype(jnp.int32), 0), narrow)
            high, low = split(a_ref[n, slot * edge : (slot + 1) * edge, :])
            target = pl.ds(pl.multiple_of(line * edge, edge), edge)
            left_high[target, at : at + edge] = high
            left_low[target, at : at + edge] = low
    dot = functools.partial(jnp.dot, preferred_element_type=jnp.float32)
    for m in range(0, width, 2):
        columns = slice(m * edge, (m + 2) * edge)
        value = (
            dot(left_high[...], right_high[:, columns])
            + dot(left_low[...], right_high[:, columns])
            + dot(left_high[...], right_low[:, columns])
        )
        for l in range(RL):
            for k in range(2):
                at = l * width + m + k
                piece = value[l * edge : (l + 1) * edge, k * edge : (k + 1) * edge]
                out_ref[at] = start_ref[at] + piece if has_start else piece


def product(narrow, wide, change, crossings, shares, seconds, start=None, outer=tuple(range(CL)), after=None):
    edge = shares[0][0].shape[1]
    items = len(shares)
    choices = len(shares[0])
    slots = (shares[0][0].shape[0] - PAD) // edge
    depth = items * slots * edge
    anywhere = pl.BlockSpec(memory_space=pl.ANY)
    whole = pl.BlockSpec(memory_space=pltpu.VMEM)
    places = (KBLOCKS // narrow + 2) * CL
    empty = jnp.full((places,), seconds[0].shape[0] // edge, jnp.int32)
    operands = [seconds[crossing] for crossing in sorted(set(crossings))]
    afters = [] if after is None else [after]
    if start is not None:
        operands.append(start)
    return pl.pallas_call(
        functools.partial(product_kernel, edge, slots, narrow, wide, change, choices, crossings, outer, start is not None, len(afters)),
        out_shape=jax.ShapeDtypeStruct((RL * len(outer), edge, edge), jnp.float32),
        in_specs=[anywhere] * (len(afters) + 1 + items * choices) + [whole] * len(operands),
        out_specs=whole,
        scratch_shapes=[
            pltpu.VMEM((items, slots * edge, edge), jnp.float32),
            pltpu.SMEM((items, PAD, edge), jnp.float32),
            pltpu.SMEM((2, PAD, edge), jnp.float32),
            pltpu.SMEM((2, places), jnp.int32),
            pltpu.VMEM((RL * edge, depth), jnp.bfloat16),
            pltpu.VMEM((RL * edge, depth), jnp.bfloat16),
            pltpu.VMEM((depth, len(outer) * edge), jnp.bfloat16),
            pltpu.VMEM((depth, len(outer) * edge), jnp.bfloat16),
            pltpu.SemaphoreType.DMA((items,)),
            pltpu.SemaphoreType.DMA((items,)),
            pltpu.SemaphoreType.DMA((2,)),
            pltpu.SemaphoreType.DMA((2,)),
        ],
        compiler_params=pltpu.CompilerParams(vmem_limit_bytes=VMEM_LIMIT),
        cost_estimate=pl.CostEstimate(
            flops=6 * RL * depth * len(outer) * edge * edge, bytes_accessed=4 * 1024 * 1024, transcendentals=0
        ),
    )(*afters, empty, *[ref for share in shares for ref in share], *operands)


def share_kernel(*refs):
    arrays = len(refs) // 7
    parts = [refs[n * arrays : (n + 1) * arrays] for n in range(7)]
    waits = []
    for blocks_hbm, index_hbm, out_hbm, tile_ref, index_ref, block_sem, index_sem in zip(*parts):
        slots, edge, _ = blocks_hbm.shape
        copies = [
            pltpu.make_async_copy(blocks_hbm.at[slot], out_hbm.at[pl.ds(slot * edge, edge)], block_sem.at[slot])
            for slot in range(slots)
        ]
        index_copy = pltpu.make_async_copy(index_hbm, index_ref, index_sem)
        index_copy.start()
        for copy in copies:
            copy.start()
        waits += copies
    for blocks_hbm, index_hbm, out_hbm, tile_ref, index_ref, block_sem, index_sem in zip(*parts):
        slots, edge, _ = blocks_hbm.shape
        pltpu.make_async_copy(index_hbm, index_ref, index_sem).wait()
        shape = tile_ref.shape
        row = lax.broadcasted_iota(jnp.int32, shape, 0)
        column = lax.broadcasted_iota(jnp.int32, shape, 1)
        tile = jnp.zeros(shape, jnp.float32)
        for n in range(2):
            for slot in range(slots):
                tile = jnp.where((row == n) & (column == slot), index_ref[0, n, slot].astype(jnp.float32), tile)
        tile_ref[...] = tile
        tile_copy = pltpu.make_async_copy(tile_ref, out_hbm.at[pl.ds(slots * edge, PAD)], block_sem.at[slots])
        tile_copy.start()
        waits.append(tile_copy)
    for copy in waits:
        copy.wait()


def build_shares(blocks, indices):
    anywhere = pl.BlockSpec(memory_space=pl.ANY)
    return pl.pallas_call(
        share_kernel,
        out_shape=tuple(
            jax.ShapeDtypeStruct((value.shape[0] * value.shape[1] + PAD, value.shape[2]), jnp.float32) for value in blocks
        ),
        in_specs=[anywhere] * (2 * len(blocks)),
        out_specs=(anywhere,) * len(blocks),
        scratch_shapes=[pltpu.VMEM((PAD, value.shape[2]), jnp.float32) for value in blocks]
        + [pltpu.SMEM(value.shape, jnp.int32) for value in indices]
        + [pltpu.SemaphoreType.DMA((value.shape[0] + 1,)) for value in blocks]
        + [pltpu.SemaphoreType.DMA for _ in blocks],
        compiler_params=pltpu.CompilerParams(vmem_limit_bytes=1024 * 1024),
    )(*[pltpu.with_memory_space_constraint(value, pltpu.HBM) for value in (*blocks, *indices)])


def local(a_blocks, a_index, b_blocks, b_index):
    narrow = lax.axis_size("narrow")
    wide = lax.axis_size("wide")
    groups = narrow // 2
    planes = wide // 2
    slots = a_blocks.shape[1]
    edge = a_blocks.shape[-1]

    def permute(name, value, to):
        pairs = []
        for r in range(narrow):
            for c in range(wide):
                target = to(r, c)
                if target is not None:
                    pairs.append((c * narrow + r, target[1] * narrow + target[0]))
        with jax.named_scope(name):
            return lax.ppermute(value, AXES, pairs)

    def swap(name, value):
        return permute(name, value, lambda r, c: (r, c ^ 1))

    share, second = build_shares((a_blocks[0], b_blocks[0]), (a_index, b_index))
    second_other = permute("second", second, lambda r, c: (r ^ 1, c))

    def spread(half, share, turn):
        def to(r, c):
            plane = c // 2
            u = plane % groups
            change = (r // 2) ^ u
            return (u * 2 + r % 2, (plane ^ change ^ turn) * 2 + c % 2)
        return permute(f"share_{half}_{turn}", share, to)

    far = permute("far", share, lambda r, c: (r, (c // 2 ^ groups) * 2 + c % 2))
    turns = [[spread(half, value, turn) for turn in range(groups)] for half, value in enumerate((share, far))]
    swapped = [[swap(f"swap_{half}", value) for value in values] for half, values in enumerate(turns)]
    candidates = [[ref for pair in zip(*values) for ref in pair] for values in zip(turns, swapped)]
    seconds = (second, second_other)
    received = []
    for change in range(1, groups):
        near, other = candidates
        first, rest = tuple(range(CL // 2)), tuple(range(CL // 2, CL))
        early = product(narrow, wide, change, (0,), [near], seconds, outer=first)
        pieces = [
            product(narrow, wide, change, (0, 1, 1), [other, near, other], seconds, early, outer=first),
            product(narrow, wide, change, (0, 0, 1, 1), [near, other] * 2, seconds, outer=rest, after=early),
        ]
        pieces = [permute(f"window_{change}", value, lambda r, c: (r ^ (change * 2), c)) for value in pieces]
        pieces = [value.reshape(RL, CL // 2, edge, edge) for value in pieces]
        received.append(jnp.concatenate(pieces, axis=1))
    total = product(narrow, wide, 0, (0, 0), candidates, seconds)
    total = product(narrow, wide, 0, (1, 1), candidates, seconds, total).reshape(RL, CL, edge, edge)
    for value in received:
        total = total + value
    return total.reshape(1, RL, 1, CL, edge, edge)


def solution(mesh):
    return jax.shard_map(
        local,
        mesh=mesh,
        in_specs=(
            P("narrow", "wide", None, None),
            P("narrow", None, "wide"),
            P("narrow", "wide", None, None),
            P("narrow", None, "wide"),
        ),
        out_specs=P("narrow", None, "wide", None, None, None),
        check_vma=False,
    )
```

```python
import functools

import jax
import jax.numpy as jnp
from jax import lax
from jax.experimental import pallas as pl
from jax.experimental.pallas import tpu as pltpu
from jax.sharding import PartitionSpec as P

RL = 2
CL = 4
KBLOCKS = 1024
PAD = 8
CHUNK = 4
AXES = ("wide", "narrow")
VMEM_LIMIT = 20 * 1024 * 1024


def split(value):
    high = value.astype(jnp.bfloat16)
    low = (value - high.astype(jnp.float32)).astype(jnp.bfloat16)
    return high, low


def product_kernel(edge, slots, narrow, wide, change, choices, crossings, outer, has_start, afters, *refs):
    width = len(outer)
    items = len(crossings)
    classes = sorted(set(crossings))
    empty_ref, refs = refs[afters], refs[afters + 1 :]
    shares = [refs[n * choices : (n + 1) * choices] for n in range(items)]
    refs = refs[items * choices :]
    second_refs, refs = dict(zip(classes, refs)), refs[len(classes) :]
    if has_start:
        start_ref, refs = refs[0], refs[1:]
    (out_ref, a_ref, index_ref, second_index, tables, found_ref, left_high, left_low, right_high, right_low,
     block_sems, index_sems, second_sems, table_sems) = refs
    row, column = lax.axis_index("narrow"), lax.axis_index("wide")
    turn = (row // 2) ^ (column // 2 % (choices // 2)) ^ change
    rows = slots * edge
    slots_second = second_refs[classes[0]].shape[0] // edge
    table_copies = []
    for crossing in classes:
        tile = pl.ds(slots_second * edge, PAD)
        table_copies.append(
            pltpu.make_async_copy(second_refs[crossing].at[tile], second_index.at[crossing], second_sems.at[crossing])
        )
        table_copies.append(pltpu.make_async_copy(empty_ref, tables.at[crossing], table_sems.at[crossing]))

    def copies(n, ref):
        return (
            pltpu.make_async_copy(ref.at[pl.ds(rows, PAD)], index_ref.at[n], index_sems.at[n]),
            pltpu.make_async_copy(ref.at[pl.ds(0, rows)], a_ref.at[pl.ds(n * rows, rows)], block_sems.at[n]),
        )

    for copy in table_copies:
        copy.start()
    for n, crossing in enumerate(crossings):
        pick = turn * 2 + ((row ^ column) % 2 ^ crossing)
        for choice in range(choices):
            @pl.when(pick == choice)
            def _():
                for copy in copies(n, shares[n][choice]):
                    copy.start()
    for copy in table_copies:
        copy.wait()
    for crossing in classes:
        for slot in range(slots_second):
            inner = second_index[crossing, 0, slot].astype(jnp.int32)
            across = second_index[crossing, 1, slot].astype(jnp.int32)
            place = lax.div(jnp.maximum(inner, 0), narrow) * CL + lax.div(jnp.maximum(across, 0), wide)
            tables[crossing, jnp.where(inner < 0, (KBLOCKS // narrow + 1) * CL, place)] = slot
    waits = [copies(n, shares[n][0]) for n in range(items)]
    for index_copy, _ in waits:
        index_copy.wait()
    for n in range(RL * width):
        out_ref[n] = start_ref[n] if has_start else jnp.zeros((edge, edge), jnp.float32)
    counts = {}
    for crossing in classes:
        count = jnp.int32(0)
        for n in range(items):
            if crossings[n] != crossing:
                continue
            for slot in range(slots):
                inner = index_ref[n, 1, slot].astype(jnp.int32)
                inner = jnp.where(inner < 0, KBLOCKS // narrow, lax.div(jnp.maximum(inner, 0), narrow))
                least = tables[crossing, inner * CL + outer[0]]
                for m in outer[1:]:
                    least = jnp.minimum(least, tables[crossing, inner * CL + m])
                found_ref[crossing, 0, count] = n * slots + slot
                found_ref[crossing, 1, count] = inner
                found_ref[crossing, 2, count] = lax.div(jnp.maximum(index_ref[n, 0, slot].astype(jnp.int32), 0), narrow)
                count = count + (least < slots_second).astype(jnp.int32)
        counts[crossing] = count
    for _, block_copy in waits:
        block_copy.wait()
    dot = functools.partial(jnp.dot, preferred_element_type=jnp.float32)

    def multiply(crossing, first):
        for k in range(CHUNK):
            there = first + k < counts[crossing]
            at = k * edge
            place = jnp.where(there, found_ref[crossing, 0, first + k], 0)
            inner = jnp.where(there, found_ref[crossing, 1, first + k], KBLOCKS // narrow)
            line = jnp.where(there, found_ref[crossing, 2, first + k], 0)
            for at_column, m in enumerate(outer):
                block = tables[crossing, inner * CL + m]
                source = pl.ds(pl.multiple_of(jnp.minimum(block, slots_second - 1) * edge, edge), edge)
                high, low = split(jnp.where(block < slots_second, second_refs[crossing][source, :], 0.0))
                right_high[at : at + edge, at_column * edge : (at_column + 1) * edge] = high
                right_low[at : at + edge, at_column * edge : (at_column + 1) * edge] = low
            high, low = split(a_ref[pl.ds(pl.multiple_of(place * edge, edge), edge), :])
            zero = jnp.zeros_like(high)
            for l in range(RL):
                left_high[l * edge : (l + 1) * edge, at : at + edge] = jnp.where(line == l, high, zero)
                left_low[l * edge : (l + 1) * edge, at : at + edge] = jnp.where(line == l, low, zero)
        for m in range(0, width, 2):
            columns = slice(m * edge, (m + 2) * edge)
            value = (
                dot(left_high[...], right_high[:, columns])
                + dot(left_low[...], right_high[:, columns])
                + dot(left_high[...], right_low[:, columns])
            )
            for l in range(RL):
                for k in range(2):
                    at = l * width + m + k
                    out_ref[at] += value[l * edge : (l + 1) * edge, k * edge : (k + 1) * edge]

    for crossing in classes:
        for first in range(0, crossings.count(crossing) * slots, CHUNK):
            @pl.when(first < counts[crossing])
            def _():
                multiply(crossing, first)


def product(narrow, wide, change, crossings, shares, seconds, start=None, outer=tuple(range(CL)), after=None):
    edge = shares[0][0].shape[1]
    items = len(shares)
    choices = len(shares[0])
    slots = (shares[0][0].shape[0] - PAD) // edge
    depth = items * slots * edge
    anywhere = pl.BlockSpec(memory_space=pl.ANY)
    whole = pl.BlockSpec(memory_space=pltpu.VMEM)
    places = (KBLOCKS // narrow + 2) * CL
    empty = jnp.full((places,), seconds[0].shape[0] // edge, jnp.int32)
    operands = [seconds[crossing] for crossing in sorted(set(crossings))]
    afters = [] if after is None else [after]
    if start is not None:
        operands.append(start)
    return pl.pallas_call(
        functools.partial(product_kernel, edge, slots, narrow, wide, change, choices, crossings, outer, start is not None, len(afters)),
        out_shape=jax.ShapeDtypeStruct((RL * len(outer), edge, edge), jnp.float32),
        in_specs=[anywhere] * (len(afters) + 1 + items * choices) + [whole] * len(operands),
        out_specs=whole,
        scratch_shapes=[
            pltpu.VMEM((depth, edge), jnp.float32),
            pltpu.SMEM((items, PAD, edge), jnp.float32),
            pltpu.SMEM((2, PAD, edge), jnp.float32),
            pltpu.SMEM((2, places), jnp.int32),
            pltpu.SMEM((2, 3, items * slots + CHUNK), jnp.int32),
            pltpu.VMEM((RL * edge, CHUNK * edge), jnp.bfloat16),
            pltpu.VMEM((RL * edge, CHUNK * edge), jnp.bfloat16),
            pltpu.VMEM((CHUNK * edge, len(outer) * edge), jnp.bfloat16),
            pltpu.VMEM((CHUNK * edge, len(outer) * edge), jnp.bfloat16),
            pltpu.SemaphoreType.DMA((items,)),
            pltpu.SemaphoreType.DMA((items,)),
            pltpu.SemaphoreType.DMA((2,)),
            pltpu.SemaphoreType.DMA((2,)),
        ],
        compiler_params=pltpu.CompilerParams(vmem_limit_bytes=VMEM_LIMIT),
        cost_estimate=pl.CostEstimate(
            flops=6 * RL * depth * len(outer) * edge * edge, bytes_accessed=4 * 1024 * 1024, transcendentals=0
        ),
    )(*afters, empty, *[ref for share in shares for ref in share], *operands)


def share_kernel(*refs):
    arrays = len(refs) // 7
    parts = [refs[n * arrays : (n + 1) * arrays] for n in range(7)]
    waits = []
    for blocks_hbm, index_hbm, out_hbm, tile_ref, index_ref, block_sem, index_sem in zip(*parts):
        slots, edge, _ = blocks_hbm.shape
        copies = [
            pltpu.make_async_copy(blocks_hbm.at[slot], out_hbm.at[pl.ds(slot * edge, edge)], block_sem.at[slot])
            for slot in range(slots)
        ]
        index_copy = pltpu.make_async_copy(index_hbm, index_ref, index_sem)
        index_copy.start()
        for copy in copies:
            copy.start()
        waits += copies
    for blocks_hbm, index_hbm, out_hbm, tile_ref, index_ref, block_sem, index_sem in zip(*parts):
        slots, edge, _ = blocks_hbm.shape
        pltpu.make_async_copy(index_hbm, index_ref, index_sem).wait()
        shape = tile_ref.shape
        row = lax.broadcasted_iota(jnp.int32, shape, 0)
        column = lax.broadcasted_iota(jnp.int32, shape, 1)
        tile = jnp.zeros(shape, jnp.float32)
        for n in range(2):
            for slot in range(slots):
                tile = jnp.where((row == n) & (column == slot), index_ref[0, n, slot].astype(jnp.float32), tile)
        tile_ref[...] = tile
        tile_copy = pltpu.make_async_copy(tile_ref, out_hbm.at[pl.ds(slots * edge, PAD)], block_sem.at[slots])
        tile_copy.start()
        waits.append(tile_copy)
    for copy in waits:
        copy.wait()


def build_shares(blocks, indices):
    anywhere = pl.BlockSpec(memory_space=pl.ANY)
    return pl.pallas_call(
        share_kernel,
        out_shape=tuple(
            jax.ShapeDtypeStruct((value.shape[0] * value.shape[1] + PAD, value.shape[2]), jnp.float32) for value in blocks
        ),
        in_specs=[anywhere] * (2 * len(blocks)),
        out_specs=(anywhere,) * len(blocks),
        scratch_shapes=[pltpu.VMEM((PAD, value.shape[2]), jnp.float32) for value in blocks]
        + [pltpu.SMEM(value.shape, jnp.int32) for value in indices]
        + [pltpu.SemaphoreType.DMA((value.shape[0] + 1,)) for value in blocks]
        + [pltpu.SemaphoreType.DMA for _ in blocks],
        compiler_params=pltpu.CompilerParams(vmem_limit_bytes=1024 * 1024),
    )(*[pltpu.with_memory_space_constraint(value, pltpu.HBM) for value in (*blocks, *indices)])


def local(a_blocks, a_index, b_blocks, b_index):
    narrow = lax.axis_size("narrow")
    wide = lax.axis_size("wide")
    groups = narrow // 2
    planes = wide // 2
    slots = a_blocks.shape[1]
    edge = a_blocks.shape[-1]

    def permute(name, value, to):
        pairs = []
        for r in range(narrow):
            for c in range(wide):
                target = to(r, c)
                if target is not None:
                    pairs.append((c * narrow + r, target[1] * narrow + target[0]))
        with jax.named_scope(name):
            return lax.ppermute(value, AXES, pairs)

    def swap(name, value):
        return permute(name, value, lambda r, c: (r, c ^ 1))

    share, second = build_shares((a_blocks[0], b_blocks[0]), (a_index, b_index))
    second_other = permute("second", second, lambda r, c: (r ^ 1, c))

    def spread(half, share, turn):
        def to(r, c):
            plane = c // 2
            u = plane % groups
            change = (r // 2) ^ u
            return (u * 2 + r % 2, (plane ^ change ^ turn) * 2 + c % 2)
        return permute(f"share_{half}_{turn}", share, to)

    far = permute("far", share, lambda r, c: (r, (c // 2 ^ groups) * 2 + c % 2))
    turns = [[spread(half, value, turn) for turn in range(groups)] for half, value in enumerate((share, far))]
    swapped = [[swap(f"swap_{half}", value) for value in values] for half, values in enumerate(turns)]
    candidates = [[ref for pair in zip(*values) for ref in pair] for values in zip(turns, swapped)]
    seconds = (second, second_other)
    received = []
    for change in range(1, groups):
        near, other = candidates
        first, rest = tuple(range(CL // 2)), tuple(range(CL // 2, CL))
        early = product(narrow, wide, change, (0,), [near], seconds, outer=first)
        pieces = [
            product(narrow, wide, change, (0, 1, 1), [other, near, other], seconds, early, outer=first),
            product(narrow, wide, change, (0, 0, 1, 1), [near, other] * 2, seconds, outer=rest, after=early),
        ]
        pieces = [permute(f"window_{change}", value, lambda r, c: (r ^ (change * 2), c)) for value in pieces]
        pieces = [value.reshape(RL, CL // 2, edge, edge) for value in pieces]
        received.append(jnp.concatenate(pieces, axis=1))
    total = product(narrow, wide, 0, (0, 0), candidates, seconds)
    total = product(narrow, wide, 0, (1, 1), candidates, seconds, total).reshape(RL, CL, edge, edge)
    for value in received:
        total = total + value
    return total.reshape(1, RL, 1, CL, edge, edge)


def solution(mesh):
    return jax.shard_map(
        local,
        mesh=mesh,
        in_specs=(
            P("narrow", "wide", None, None),
            P("narrow", None, "wide"),
            P("narrow", "wide", None, None),
            P("narrow", None, "wide"),
        ),
        out_specs=P("narrow", None, "wide", None, None, None),
        check_vma=False,
    )
```

```python
import functools

import jax
import jax.numpy as jnp
from jax import lax
from jax.experimental import pallas as pl
from jax.experimental.pallas import tpu as pltpu
from jax.sharding import PartitionSpec as P

RL = 2
CL = 4
KBLOCKS = 1024
PAD = 8
AXES = ("wide", "narrow")
VMEM_LIMIT = 20 * 1024 * 1024


def split(value):
    high = value.astype(jnp.bfloat16)
    low = (value - high.astype(jnp.float32)).astype(jnp.bfloat16)
    return high, low


def product_kernel(edge, slots, narrow, wide, change, choices, crossings, outer, has_start, afters, *refs):
    width = len(outer)
    items = len(crossings)
    classes = sorted(set(crossings))
    empty_ref, refs = refs[afters], refs[afters + 1 :]
    shares = [refs[n * choices : (n + 1) * choices] for n in range(items)]
    refs = refs[items * choices :]
    second_refs, refs = dict(zip(classes, refs)), refs[len(classes) :]
    if has_start:
        start_ref, refs = refs[0], refs[1:]
    (out_ref, a_ref, index_ref, second_index, tables, left_high, left_low, right_high, right_low,
     block_sems, index_sems, second_sems, table_sems) = refs
    row, column = lax.axis_index("narrow"), lax.axis_index("wide")
    turn = (row // 2) ^ (column // 2 % (choices // 2)) ^ change
    rows = slots * edge
    slots_second = second_refs[classes[0]].shape[0] // edge
    table_copies = []
    for crossing in classes:
        tile = pl.ds(slots_second * edge, PAD)
        table_copies.append(
            pltpu.make_async_copy(second_refs[crossing].at[tile], second_index.at[crossing], second_sems.at[crossing])
        )
        table_copies.append(pltpu.make_async_copy(empty_ref, tables.at[crossing], table_sems.at[crossing]))

    def copies(n, ref):
        return (
            pltpu.make_async_copy(ref.at[pl.ds(rows, PAD)], index_ref.at[n], index_sems.at[n]),
            pltpu.make_async_copy(ref.at[pl.ds(0, rows)], a_ref.at[n], block_sems.at[n]),
        )

    for copy in table_copies:
        copy.start()
    for n, crossing in enumerate(crossings):
        pick = turn * 2 + ((row ^ column) % 2 ^ crossing)
        for choice in range(choices):
            @pl.when(pick == choice)
            def _():
                for copy in copies(n, shares[n][choice]):
                    copy.start()
    left_high[...] = jnp.zeros_like(left_high)
    left_low[...] = jnp.zeros_like(left_low)
    for copy in table_copies:
        copy.wait()
    for crossing in classes:
        for slot in range(slots_second):
            inner = second_index[crossing, 0, slot].astype(jnp.int32)
            across = second_index[crossing, 1, slot].astype(jnp.int32)
            place = lax.div(jnp.maximum(inner, 0), narrow) * CL + lax.div(jnp.maximum(across, 0), wide)
            tables[crossing, jnp.where(inner < 0, (KBLOCKS // narrow + 1) * CL, place)] = slot
    waits = [copies(n, shares[n][0]) for n in range(items)]
    for index_copy, _ in waits:
        index_copy.wait()
    for _, block_copy in waits:
        block_copy.wait()
    for n, crossing in enumerate(crossings):
        for slot in range(slots):
            at = (n * slots + slot) * edge
            inner = index_ref[n, 1, slot].astype(jnp.int32)
            inner = jnp.where(inner < 0, KBLOCKS // narrow, lax.div(jnp.maximum(inner, 0), narrow))
            for at_column, m in enumerate(outer):
                block = tables[crossing, inner * CL + m]
                source = pl.ds(pl.multiple_of(jnp.minimum(block, slots_second - 1) * edge, edge), edge)
                high, low = split(jnp.where(block < slots_second, second_refs[crossing][source, :], 0.0))
                right_high[at : at + edge, at_column * edge : (at_column + 1) * edge] = high
                right_low[at : at + edge, at_column * edge : (at_column + 1) * edge] = low
    for n in range(items):
        for slot in range(slots):
            at = (n * slots + slot) * edge
            line = lax.div(jnp.maximum(index_ref[n, 0, slot].astype(jnp.int32), 0), narrow)
            high, low = split(a_ref[n, slot * edge : (slot + 1) * edge, :])
            target = pl.ds(pl.multiple_of(line * edge, edge), edge)
            left_high[target, at : at + edge] = high
            left_low[target, at : at + edge] = low
    dot = functools.partial(jnp.dot, preferred_element_type=jnp.float32)
    for m in range(0, width, 2):
        columns = slice(m * edge, (m + 2) * edge)
        value = (
            dot(left_high[...], right_high[:, columns])
            + dot(left_low[...], right_high[:, columns])
            + dot(left_high[...], right_low[:, columns])
        )
        for l in range(RL):
            for k in range(2):
                at = l * width + m + k
                piece = value[l * edge : (l + 1) * edge, k * edge : (k + 1) * edge]
                out_ref[at] = start_ref[at] + piece if has_start else piece


def product(narrow, wide, change, crossings, shares, seconds, start=None, outer=tuple(range(CL)), after=None):
    edge = shares[0][0].shape[1]
    items = len(shares)
    choices = len(shares[0])
    slots = (shares[0][0].shape[0] - PAD) // edge
    depth = items * slots * edge
    anywhere = pl.BlockSpec(memory_space=pl.ANY)
    whole = pl.BlockSpec(memory_space=pltpu.VMEM)
    places = (KBLOCKS // narrow + 2) * CL
    empty = jnp.full((places,), seconds[0].shape[0] // edge, jnp.int32)
    operands = [seconds[crossing] for crossing in sorted(set(crossings))]
    afters = [] if after is None else [after]
    if start is not None:
        operands.append(start)
    return pl.pallas_call(
        functools.partial(product_kernel, edge, slots, narrow, wide, change, choices, crossings, outer, start is not None, len(afters)),
        out_shape=jax.ShapeDtypeStruct((RL * len(outer), edge, edge), jnp.float32),
        in_specs=[anywhere] * (len(afters) + 1 + items * choices) + [whole] * len(operands),
        out_specs=whole,
        scratch_shapes=[
            pltpu.VMEM((items, slots * edge, edge), jnp.float32),
            pltpu.SMEM((items, PAD, edge), jnp.float32),
            pltpu.SMEM((2, PAD, edge), jnp.float32),
            pltpu.SMEM((2, places), jnp.int32),
            pltpu.VMEM((RL * edge, depth), jnp.bfloat16),
            pltpu.VMEM((RL * edge, depth), jnp.bfloat16),
            pltpu.VMEM((depth, len(outer) * edge), jnp.bfloat16),
            pltpu.VMEM((depth, len(outer) * edge), jnp.bfloat16),
            pltpu.SemaphoreType.DMA((items,)),
            pltpu.SemaphoreType.DMA((items,)),
            pltpu.SemaphoreType.DMA((2,)),
            pltpu.SemaphoreType.DMA((2,)),
        ],
        compiler_params=pltpu.CompilerParams(vmem_limit_bytes=VMEM_LIMIT),
        cost_estimate=pl.CostEstimate(
            flops=6 * RL * depth * len(outer) * edge * edge, bytes_accessed=4 * 1024 * 1024, transcendentals=0
        ),
    )(*afters, empty, *[ref for share in shares for ref in share], *operands)


def share_kernel(*refs):
    arrays = len(refs) // 7
    parts = [refs[n * arrays : (n + 1) * arrays] for n in range(7)]
    waits = []
    for blocks_hbm, index_hbm, out_hbm, tile_ref, index_ref, block_sem, index_sem in zip(*parts):
        rows = blocks_hbm.shape[0]
        copies = [pltpu.make_async_copy(blocks_hbm, out_hbm.at[pl.ds(0, rows)], block_sem.at[0])]
        index_copy = pltpu.make_async_copy(index_hbm, index_ref, index_sem)
        index_copy.start()
        for copy in copies:
            copy.start()
        waits += copies
    for blocks_hbm, index_hbm, out_hbm, tile_ref, index_ref, block_sem, index_sem in zip(*parts):
        rows, slots = blocks_hbm.shape[0], index_hbm.shape[-1]
        pltpu.make_async_copy(index_hbm, index_ref, index_sem).wait()
        shape = tile_ref.shape
        row = lax.broadcasted_iota(jnp.int32, shape, 0)
        column = lax.broadcasted_iota(jnp.int32, shape, 1)
        tile = jnp.zeros(shape, jnp.float32)
        for n in range(2):
            for slot in range(slots):
                tile = jnp.where((row == n) & (column == slot), index_ref[0, n, slot].astype(jnp.float32), tile)
        tile_ref[...] = tile
        tile_copy = pltpu.make_async_copy(tile_ref, out_hbm.at[pl.ds(rows, PAD)], block_sem.at[1])
        tile_copy.start()
        waits.append(tile_copy)
    for copy in waits:
        copy.wait()


def build_shares(blocks, indices):
    anywhere = pl.BlockSpec(memory_space=pl.ANY)
    return pl.pallas_call(
        share_kernel,
        out_shape=tuple(
            jax.ShapeDtypeStruct((value.shape[0] + PAD, value.shape[1]), jnp.float32) for value in blocks
        ),
        in_specs=[anywhere] * (2 * len(blocks)),
        out_specs=(anywhere,) * len(blocks),
        scratch_shapes=[pltpu.VMEM((PAD, value.shape[1]), jnp.float32) for value in blocks]
        + [pltpu.SMEM(value.shape, jnp.int32) for value in indices]
        + [pltpu.SemaphoreType.DMA((2,)) for _ in blocks]
        + [pltpu.SemaphoreType.DMA for _ in blocks],
        compiler_params=pltpu.CompilerParams(vmem_limit_bytes=1024 * 1024),
    )(*[pltpu.with_memory_space_constraint(value, pltpu.HBM) for value in (*blocks, *indices)])


def local(a_blocks, a_index, b_blocks, b_index):
    narrow = lax.axis_size("narrow")
    wide = lax.axis_size("wide")
    groups = narrow // 2
    planes = wide // 2
    slots = a_blocks.shape[1]
    edge = a_blocks.shape[-1]

    def permute(name, value, to):
        pairs = []
        for r in range(narrow):
            for c in range(wide):
                target = to(r, c)
                if target is not None:
                    pairs.append((c * narrow + r, target[1] * narrow + target[0]))
        with jax.named_scope(name):
            return lax.ppermute(value, AXES, pairs)

    def swap(name, value):
        return permute(name, value, lambda r, c: (r, c ^ 1))

    share, second = build_shares((a_blocks.reshape(-1, edge), b_blocks.reshape(-1, edge)), (a_index, b_index))
    second_other = permute("second", second, lambda r, c: (r ^ 1, c))

    def spread(half, share, turn):
        def to(r, c):
            plane = c // 2
            u = plane % groups
            change = (r // 2) ^ u
            return (u * 2 + r % 2, (plane ^ change ^ turn) * 2 + c % 2)
        return permute(f"share_{half}_{turn}", share, to)

    far = permute("far", share, lambda r, c: (r, (c // 2 ^ groups) * 2 + c % 2))
    turns = [[spread(half, value, turn) for turn in range(groups)] for half, value in enumerate((share, far))]
    swapped = [[swap(f"swap_{half}", value) for value in values] for half, values in enumerate(turns)]
    candidates = [[ref for pair in zip(*values) for ref in pair] for values in zip(turns, swapped)]
    seconds = (second, second_other)
    received = []
    for change in range(1, groups):
        near, other = candidates
        first, rest = tuple(range(CL // 2)), tuple(range(CL // 2, CL))
        early = product(narrow, wide, change, (0,), [near], seconds, outer=first)
        pieces = [
            product(narrow, wide, change, (0, 1, 1), [other, near, other], seconds, early, outer=first),
            product(narrow, wide, change, (0, 0, 1, 1), [near, other] * 2, seconds, outer=rest, after=early),
        ]
        pieces = [permute(f"window_{change}", value, lambda r, c: (r ^ (change * 2), c)) for value in pieces]
        pieces = [value.reshape(RL, CL // 2, edge, edge) for value in pieces]
        received.append(jnp.concatenate(pieces, axis=1))
    total = product(narrow, wide, 0, (0, 0), candidates, seconds)
    total = product(narrow, wide, 0, (1, 1), candidates, seconds, total).reshape(RL, CL, edge, edge)
    for value in received:
        total = total + value
    return total.reshape(1, RL, 1, CL, edge, edge)


def solution(mesh):
    return jax.shard_map(
        local,
        mesh=mesh,
        in_specs=(
            P("narrow", "wide", None, None),
            P("narrow", None, "wide"),
            P("narrow", "wide", None, None),
            P("narrow", None, "wide"),
        ),
        out_specs=P("narrow", None, "wide", None, None, None),
        check_vma=False,
    )
```

```python
import functools

import jax
import jax.numpy as jnp
from jax import lax
from jax.experimental import pallas as pl
from jax.experimental.pallas import tpu as pltpu
from jax.sharding import PartitionSpec as P

RL = 2
CL = 4
KBLOCKS = 1024
PAD = 8
CHUNK = 4
AXES = ("wide", "narrow")
VMEM_LIMIT = 20 * 1024 * 1024


def split(value):
    high = value.astype(jnp.bfloat16)
    low = (value - high.astype(jnp.float32)).astype(jnp.bfloat16)
    return high, low


def product_kernel(edge, slots, narrow, wide, change, choices, crossings, outer, has_start, afters, *refs):
    width = len(outer)
    items = len(crossings)
    classes = sorted(set(crossings))
    empty_ref, refs = refs[afters], refs[afters + 1 :]
    shares = [refs[n * choices : (n + 1) * choices] for n in range(items)]
    refs = refs[items * choices :]
    second_refs, refs = dict(zip(classes, refs)), refs[len(classes) :]
    if has_start:
        start_ref, refs = refs[0], refs[1:]
    (out_ref, a_ref, index_ref, second_index, tables, found_ref, left_high, left_low, right_high, right_low,
     block_sems, index_sems, second_sems, table_sems) = refs
    row, column = lax.axis_index("narrow"), lax.axis_index("wide")
    turn = (row // 2) ^ (column // 2 % (choices // 2)) ^ change
    rows = slots * edge
    slots_second = second_refs[classes[0]].shape[0] // edge
    table_copies = []
    for crossing in classes:
        tile = pl.ds(slots_second * edge, PAD)
        table_copies.append(
            pltpu.make_async_copy(second_refs[crossing].at[tile], second_index.at[crossing], second_sems.at[crossing])
        )
        table_copies.append(pltpu.make_async_copy(empty_ref, tables.at[crossing], table_sems.at[crossing]))

    def copies(n, ref):
        return (
            pltpu.make_async_copy(ref.at[pl.ds(rows, PAD)], index_ref.at[n], index_sems.at[n]),
            pltpu.make_async_copy(ref.at[pl.ds(0, rows)], a_ref.at[pl.ds(n * rows, rows)], block_sems.at[n]),
        )

    for copy in table_copies:
        copy.start()
    for n, crossing in enumerate(crossings):
        pick = turn * 2 + ((row ^ column) % 2 ^ crossing)
        for choice in range(choices):
            @pl.when(pick == choice)
            def _():
                for copy in copies(n, shares[n][choice]):
                    copy.start()
    for copy in table_copies:
        copy.wait()
    for crossing in classes:
        for slot in range(slots_second):
            inner = second_index[crossing, 0, slot].astype(jnp.int32)
            across = second_index[crossing, 1, slot].astype(jnp.int32)
            place = lax.div(jnp.maximum(inner, 0), narrow) * CL + lax.div(jnp.maximum(across, 0), wide)
            tables[crossing, jnp.where(inner < 0, (KBLOCKS // narrow + 1) * CL, place)] = slot
    waits = [copies(n, shares[n][0]) for n in range(items)]
    for index_copy, _ in waits:
        index_copy.wait()
    for n in range(RL * width):
        out_ref[n] = start_ref[n] if has_start else jnp.zeros((edge, edge), jnp.float32)
    counts = {}
    for crossing in classes:
        count = jnp.int32(0)
        for n in range(items):
            if crossings[n] != crossing:
                continue
            for slot in range(slots):
                inner = index_ref[n, 1, slot].astype(jnp.int32)
                inner = jnp.where(inner < 0, KBLOCKS // narrow, lax.div(jnp.maximum(inner, 0), narrow))
                least = tables[crossing, inner * CL + outer[0]]
                for m in outer[1:]:
                    least = jnp.minimum(least, tables[crossing, inner * CL + m])
                found_ref[crossing, 0, count] = n * slots + slot
                found_ref[crossing, 1, count] = inner
                found_ref[crossing, 2, count] = lax.div(jnp.maximum(index_ref[n, 0, slot].astype(jnp.int32), 0), narrow)
                count = count + (least < slots_second).astype(jnp.int32)
        counts[crossing] = count
    for _, block_copy in waits:
        block_copy.wait()
    dot = functools.partial(jnp.dot, preferred_element_type=jnp.float32)

    def multiply(crossing, first):
        for k in range(CHUNK):
            there = first + k < counts[crossing]
            at = k * edge
            place = jnp.where(there, found_ref[crossing, 0, first + k], 0)
            inner = jnp.where(there, found_ref[crossing, 1, first + k], KBLOCKS // narrow)
            line = jnp.where(there, found_ref[crossing, 2, first + k], 0)
            for at_column, m in enumerate(outer):
                block = tables[crossing, inner * CL + m]
                source = pl.ds(pl.multiple_of(jnp.minimum(block, slots_second - 1) * edge, edge), edge)
                high, low = split(jnp.where(block < slots_second, second_refs[crossing][source, :], 0.0))
                right_high[at : at + edge, at_column * edge : (at_column + 1) * edge] = high
                right_low[at : at + edge, at_column * edge : (at_column + 1) * edge] = low
            high, low = split(a_ref[pl.ds(pl.multiple_of(place * edge, edge), edge), :])
            zero = jnp.zeros_like(high)
            for l in range(RL):
                left_high[l * edge : (l + 1) * edge, at : at + edge] = jnp.where(line == l, high, zero)
                left_low[l * edge : (l + 1) * edge, at : at + edge] = jnp.where(line == l, low, zero)
        for m in range(0, width, 2):
            columns = slice(m * edge, (m + 2) * edge)
            value = (
                dot(left_high[...], right_high[:, columns])
                + dot(left_low[...], right_high[:, columns])
                + dot(left_high[...], right_low[:, columns])
            )
            for l in range(RL):
                for k in range(2):
                    at = l * width + m + k
                    out_ref[at] += value[l * edge : (l + 1) * edge, k * edge : (k + 1) * edge]

    for crossing in classes:
        for first in range(0, crossings.count(crossing) * slots, CHUNK):
            @pl.when(first < counts[crossing])
            def _():
                multiply(crossing, first)


def product(narrow, wide, change, crossings, shares, seconds, start=None, outer=tuple(range(CL)), after=None):
    edge = shares[0][0].shape[1]
    items = len(shares)
    choices = len(shares[0])
    slots = (shares[0][0].shape[0] - PAD) // edge
    depth = items * slots * edge
    anywhere = pl.BlockSpec(memory_space=pl.ANY)
    whole = pl.BlockSpec(memory_space=pltpu.VMEM)
    places = (KBLOCKS // narrow + 2) * CL
    empty = jnp.full((places,), seconds[0].shape[0] // edge, jnp.int32)
    operands = [seconds[crossing] for crossing in sorted(set(crossings))]
    afters = [] if after is None else [after]
    if start is not None:
        operands.append(start)
    return pl.pallas_call(
        functools.partial(product_kernel, edge, slots, narrow, wide, change, choices, crossings, outer, start is not None, len(afters)),
        out_shape=jax.ShapeDtypeStruct((RL * len(outer), edge, edge), jnp.float32),
        in_specs=[anywhere] * (len(afters) + 1 + items * choices) + [whole] * len(operands),
        out_specs=whole,
        scratch_shapes=[
            pltpu.VMEM((depth, edge), jnp.float32),
            pltpu.SMEM((items, PAD, edge), jnp.float32),
            pltpu.SMEM((2, PAD, edge), jnp.float32),
            pltpu.SMEM((2, places), jnp.int32),
            pltpu.SMEM((2, 3, items * slots + CHUNK), jnp.int32),
            pltpu.VMEM((RL * edge, CHUNK * edge), jnp.bfloat16),
            pltpu.VMEM((RL * edge, CHUNK * edge), jnp.bfloat16),
            pltpu.VMEM((CHUNK * edge, len(outer) * edge), jnp.bfloat16),
            pltpu.VMEM((CHUNK * edge, len(outer) * edge), jnp.bfloat16),
            pltpu.SemaphoreType.DMA((items,)),
            pltpu.SemaphoreType.DMA((items,)),
            pltpu.SemaphoreType.DMA((2,)),
            pltpu.SemaphoreType.DMA((2,)),
        ],
        compiler_params=pltpu.CompilerParams(vmem_limit_bytes=VMEM_LIMIT),
        cost_estimate=pl.CostEstimate(
            flops=6 * RL * depth * len(outer) * edge * edge, bytes_accessed=4 * 1024 * 1024, transcendentals=0
        ),
    )(*afters, empty, *[ref for share in shares for ref in share], *operands)


def share_kernel(*refs):
    arrays = len(refs) // 7
    parts = [refs[n * arrays : (n + 1) * arrays] for n in range(7)]
    waits = []
    for blocks_hbm, index_hbm, out_hbm, tile_ref, index_ref, block_sem, index_sem in zip(*parts):
        rows = blocks_hbm.shape[0]
        copies = [pltpu.make_async_copy(blocks_hbm, out_hbm.at[pl.ds(0, rows)], block_sem.at[0])]
        index_copy = pltpu.make_async_copy(index_hbm, index_ref, index_sem)
        index_copy.start()
        for copy in copies:
            copy.start()
        waits += copies
    for blocks_hbm, index_hbm, out_hbm, tile_ref, index_ref, block_sem, index_sem in zip(*parts):
        rows, slots = blocks_hbm.shape[0], index_hbm.shape[-1]
        pltpu.make_async_copy(index_hbm, index_ref, index_sem).wait()
        shape = tile_ref.shape
        row = lax.broadcasted_iota(jnp.int32, shape, 0)
        column = lax.broadcasted_iota(jnp.int32, shape, 1)
        tile = jnp.zeros(shape, jnp.float32)
        for n in range(2):
            for slot in range(slots):
                tile = jnp.where((row == n) & (column == slot), index_ref[0, n, slot].astype(jnp.float32), tile)
        tile_ref[...] = tile
        tile_copy = pltpu.make_async_copy(tile_ref, out_hbm.at[pl.ds(rows, PAD)], block_sem.at[1])
        tile_copy.start()
        waits.append(tile_copy)
    for copy in waits:
        copy.wait()


def build_shares(blocks, indices):
    anywhere = pl.BlockSpec(memory_space=pl.ANY)
    return pl.pallas_call(
        share_kernel,
        out_shape=tuple(
            jax.ShapeDtypeStruct((value.shape[0] + PAD, value.shape[1]), jnp.float32) for value in blocks
        ),
        in_specs=[anywhere] * (2 * len(blocks)),
        out_specs=(anywhere,) * len(blocks),
        scratch_shapes=[pltpu.VMEM((PAD, value.shape[1]), jnp.float32) for value in blocks]
        + [pltpu.SMEM(value.shape, jnp.int32) for value in indices]
        + [pltpu.SemaphoreType.DMA((2,)) for _ in blocks]
        + [pltpu.SemaphoreType.DMA for _ in blocks],
        compiler_params=pltpu.CompilerParams(vmem_limit_bytes=1024 * 1024),
    )(*[pltpu.with_memory_space_constraint(value, pltpu.HBM) for value in (*blocks, *indices)])


def local(a_blocks, a_index, b_blocks, b_index):
    narrow = lax.axis_size("narrow")
    wide = lax.axis_size("wide")
    groups = narrow // 2
    planes = wide // 2
    slots = a_blocks.shape[1]
    edge = a_blocks.shape[-1]

    def permute(name, value, to):
        pairs = []
        for r in range(narrow):
            for c in range(wide):
                target = to(r, c)
                if target is not None:
                    pairs.append((c * narrow + r, target[1] * narrow + target[0]))
        with jax.named_scope(name):
            return lax.ppermute(value, AXES, pairs)

    def swap(name, value):
        return permute(name, value, lambda r, c: (r, c ^ 1))

    share, second = build_shares((a_blocks.reshape(-1, edge), b_blocks.reshape(-1, edge)), (a_index, b_index))
    second_other = permute("second", second, lambda r, c: (r ^ 1, c))

    def spread(half, share, turn):
        def to(r, c):
            plane = c // 2
            u = plane % groups
            change = (r // 2) ^ u
            return (u * 2 + r % 2, (plane ^ change ^ turn) * 2 + c % 2)
        return permute(f"share_{half}_{turn}", share, to)

    far = permute("far", share, lambda r, c: (r, (c // 2 ^ groups) * 2 + c % 2))
    turns = [[spread(half, value, turn) for turn in range(groups)] for half, value in enumerate((share, far))]
    swapped = [[swap(f"swap_{half}", value) for value in values] for half, values in enumerate(turns)]
    candidates = [[ref for pair in zip(*values) for ref in pair] for values in zip(turns, swapped)]
    seconds = (second, second_other)
    received = []
    for change in range(1, groups):
        near, other = candidates
        first, rest = tuple(range(CL // 2)), tuple(range(CL // 2, CL))
        early = product(narrow, wide, change, (0,), [near], seconds, outer=first)
        pieces = [
            product(narrow, wide, change, (0, 1, 1), [other, near, other], seconds, early, outer=first),
            product(narrow, wide, change, (0, 0, 1, 1), [near, other] * 2, seconds, outer=rest, after=early),
        ]
        pieces = [permute(f"window_{change}", value, lambda r, c: (r ^ (change * 2), c)) for value in pieces]
        pieces = [value.reshape(RL, CL // 2, edge, edge) for value in pieces]
        received.append(jnp.concatenate(pieces, axis=1))
    total = product(narrow, wide, 0, (0, 0), candidates, seconds)
    total = product(narrow, wide, 0, (1, 1), candidates, seconds, total).reshape(RL, CL, edge, edge)
    for value in received:
        total = total + value
    return total.reshape(1, RL, 1, CL, edge, edge)


def solution(mesh):
    return jax.shard_map(
        local,
        mesh=mesh,
        in_specs=(
            P("narrow", "wide", None, None),
            P("narrow", None, "wide"),
            P("narrow", "wide", None, None),
            P("narrow", None, "wide"),
        ),
        out_specs=P("narrow", None, "wide", None, None, None),
        check_vma=False,
    )
```
